32 devices in a mesh: section: 4 (over y, core), expert: 4 (over z), tensor: 2 (over x).
Axes of the slice: x: 2, y: 2, z: 4, core: 2. Of those that a mesh axis runs over, the one named last changes fastest.
Arguments:
- tokens: bfloat16 [4, 1024, 2048], P('section', ('expert', 'tensor')), may hold values from -6 to 6
- routes: int32 [4, 1024, 2], P('section', ('expert', 'tensor')), may hold values from 0 to 3, all different within a row; in each aligned block of 128 rows (0 to 127, 128 to 255, ..., all dimensions but the last counted through in order) at most 128 rows name the same one
- route_weights: float32 [4, 1024, 2], P('section', ('expert', 'tensor')), may hold values from 0.2 to 1
- expert_gate: bfloat16 [4, 4, 2048, 512], P('section', 'expert'), may hold values from -0.125 to 0.125
- expert_up: bfloat16 [4, 4, 2048, 512], P('section', 'expert'), may hold values from -0.125 to 0.125
- expert_down: bfloat16 [4, 4, 512, 2048], P('section', 'expert'), may hold values from -0.25 to 0.25
Outputs:
- layer_out: bfloat16 [4, 1024, 2048], P('section', ('expert', 'tensor'))
- next_input: bfloat16 [4, 1024, 2048], P('section', ('expert', 'tensor'))
The draws below stay inside these ranges and needn't reach their ends.
Inputs may be any that keep to these rules, and one draw needn't show every extreme that they name: Each token names 2 different experts; among the tokens of one device no expert is named by more than 128 routes, a bound that some block reaches.
All inputs are finite; a program needn't handle non-finite values.
Results may differ from the reference program's by a relative error of at most 0.0042.
Values may be sent and summed in bfloat16 or wider, within the bound.
No kernel may reach another device: no remote copies, remote signals or barrier semaphores. Data moves between devices by JAX's collectives and lax.ppermute only.
A program may use at most 64 MiB of HBM per device.

```python
import math
import jax
import jax.numpy as jnp
import numpy as np
from jax import lax

D = 2048
FF = 512
TOPK = 2
TOK_DEV = 128
EXPERTS = 4
CAP = 128
TOKENS = 1024
N_SECTION = 4
N_EXPERT = 4
N_TENSOR = 2


def shard_levels(rng, shape, shards, low, high):
    factor_of = 1.0
    for dim, blocks in shards:
        draws = jax.random.uniform(jax.random.fold_in(jax.random.fold_in(rng, 6), dim), (blocks,), jnp.float32, low / len(shards), high / len(shards))
        factor_of = factor_of * jnp.repeat(jnp.exp(draws), shape[dim] // blocks).reshape((-1,) + (1,) * (len(shape) - 1 - dim))
    return factor_of


def routed_block(rng, own, number, rows, amount, top, reach, lean):
    sequence = jax.random.permutation(rng, amount)
    heavy_load, ordinary = portions_of(amount, rows * top, reach, lean, True), portions_of(amount, rows * top, reach, lean, False)
    places = jnp.arange(amount)

    def named(sizes, rotation):
        used = int((sizes > 0).sum())
        fixed = max(1, used // 4)
        shifted = fixed + (places - fixed + rotation * (used - fixed)) % max(1, amount - fixed)
        return jnp.zeros((amount,), jnp.int32).at[sequence[jnp.where(places < fixed, places, shifted)]].set(jnp.asarray(sizes, jnp.int32))

    sizes = jnp.where(number % 4 == 0, named(heavy_load, number // 4), named(ordinary, number - number // 4 - 1))
    mixed = jax.random.permutation(jax.random.fold_in(own, 3), amount)
    source_of, taker = mixed[0:amount // 2 * 2:2], mixed[1:amount // 2 * 2:2]
    room = jnp.minimum(sizes[source_of] - 1, reach - sizes[taker]) // 2
    room = jnp.where((source_of == sequence[0]) | (taker == sequence[0]) | (sizes[taker] == 0), 0, jnp.maximum(room, 0))
    shifted = jax.random.randint(jax.random.fold_in(own, 4), (amount // 2,), 0, 1 << 20) % (room + 1)
    sizes = sizes.at[source_of].add(-shifted).at[taker].add(shifted)
    items = jnp.searchsorted(jnp.cumsum(sizes), jnp.arange(rows * top), side="right").astype(jnp.int32)
    table = items.reshape(top, rows).T
    table = table[jax.random.permutation(jax.random.fold_in(own, 1), rows)]
    rotation = jax.random.randint(jax.random.fold_in(own, 2), (rows, 1), 0, top)
    return jnp.take_along_axis(table, (jnp.arange(top)[None, :] + rotation) % top, axis=1)


def portions_of(count, total, reach, slope, full):
    weights = [(1 << 20) // math.isqrt(standing ** slope) + 1 for standing in range(1, count + 1)]
    largest = reach if full else min(reach, max(-(-total // count), total * weights[0] // sum(weights)))
    least = 1 if total - largest >= count - 1 else 0
    counts, spare = [largest] + [least] * (count - 1), total - largest - least * (count - 1)
    while spare > 0:
        candidates = [i for i in range(1, count) if counts[i] < largest] or [i for i in range(1, count) if counts[i] < reach]
        whole, left = sum([weights[i] for i in candidates]), spare
        for i in candidates:
            addition = min(reach - counts[i], max(1, left * weights[i] // whole), spare)
            counts[i] = counts[i] + addition
            spare = spare - addition
    return np.array(counts)


def noise(rng, dims, scale, limit, shards=(), kind=jnp.bfloat16):
    loudness = shard_levels(rng, dims, shards, -0.22, 0.18) if shards else 1.0
    values = jax.random.normal(rng, dims, jnp.float32) * scale * loudness
    return jnp.minimum(jnp.maximum(values, -limit), limit).astype(kind)


def setup_inputs(seed: int = 0) -> dict:
    key_list = jax.random.split(jax.random.key(seed), 7)
    tokens = noise(key_list[0], (N_SECTION, TOKENS, D), 1.0, 6.0, ((0, 4), (1, 8)))
    routes_keys = jax.random.split(jax.random.fold_in(key_list[1], 1), N_SECTION * TOKENS // TOK_DEV)
    routes_turns = jax.random.permutation(jax.random.fold_in(key_list[1], 3), N_SECTION * TOKENS // TOK_DEV)
    routes = jax.vmap(lambda own, number: routed_block(jax.random.fold_in(key_list[1], 2), own, number, TOK_DEV, EXPERTS, TOPK, CAP, 2))(routes_keys, routes_turns).reshape((N_SECTION, TOKENS, TOPK))
    route_weights = jnp.clip(jnp.exp(math.log(1.0) - 1.609438 * jax.random.uniform(key_list[2], (N_SECTION, TOKENS, TOPK), jnp.float32) ** shard_levels(key_list[2], (N_SECTION, TOKENS, TOPK), ((0, 4), (1, 8)), -0.2, 0.2)), 0.2, 1.0)
    expert_gate = noise(key_list[3], (N_SECTION, EXPERTS, D, FF), D ** -0.5, 0.125, ((0, 4), (1, 4)))
    expert_up = noise(key_list[4], (N_SECTION, EXPERTS, D, FF), D ** -0.5, 0.125, ((0, 4), (1, 4)))
    expert_down = noise(key_list[5], (N_SECTION, EXPERTS, FF, D), FF ** -0.5, 0.25, ((0, 4), (1, 4)))
    return {"tokens": tokens, "routes": routes, "route_weights": route_weights, "expert_gate": expert_gate, "expert_up": expert_up, "expert_down": expert_down}


def one_section(items):
    rows_in, flat_routes, flat_weights, w_gate, w_up, w_down = items
    token_of = (jnp.arange(TOKENS * TOPK, dtype=jnp.int32) // TOPK).astype(jnp.int32)
    slot_total = N_EXPERT * N_TENSOR * CAP

    def per_expert(total, packed):
        expert_id, gate_e, up_e, down_e = packed
        match = flat_routes == expert_id
        picked = jnp.nonzero(match, size=slot_total, fill_value=0)[0].astype(jnp.int32)
        live = jnp.arange(slot_total, dtype=jnp.int32) < jnp.sum(match.astype(jnp.int32))
        source = rows_in[token_of[picked]]
        gate_val = jnp.dot(source, gate_e, preferred_element_type=jnp.float32)
        up_val = jnp.dot(source, up_e, preferred_element_type=jnp.float32)
        hidden = (jax.nn.silu(gate_val) * up_val).astype(jnp.bfloat16)
        result = jnp.dot(hidden, down_e, preferred_element_type=jnp.float32).astype(jnp.bfloat16)
        scaled = jnp.where(live, flat_weights[picked], jnp.zeros_like(flat_weights[picked]))
        total = total.at[token_of[picked]].add(result.astype(jnp.float32) * scaled[:, None])
        return total, None

    start = jnp.zeros((TOKENS, D), jnp.float32)
    routed, _ = lax.scan(per_expert, start, (jnp.arange(EXPERTS, dtype=jnp.int32), w_gate, w_up, w_down))
    return (rows_in.astype(jnp.float32) + routed).astype(jnp.bfloat16)


def reference(tokens, routes, route_weights, expert_gate, expert_up, expert_down):
    layer_out = lax.map(one_section, (tokens, routes.reshape(N_SECTION, TOKENS * TOPK), route_weights.reshape(N_SECTION, TOKENS * TOPK), expert_gate, expert_up, expert_down))
    next_input = jnp.concatenate([jnp.zeros_like(layer_out[:1]), layer_out[:-1]], axis=0)
    return layer_out, next_input
```

```python
import jax
import jax.numpy as jnp
from jax import lax
from jax.sharding import PartitionSpec as P


def passed_along(value, axis, steps):
    count = lax.axis_size(axis)
    leading, last = (max(0, -steps), min(count, count - steps))
    return lax.ppermute(value, axis, [(source, source + steps) for source in range(leading, last)])


def by_slots(tokens, routes, route_weights, expert_gate, expert_up, expert_down):
    rows_in = tokens[0]
    tok_count, width = rows_in.shape
    top_count = routes.shape[2]
    flat_routes = routes[0].reshape(tok_count * top_count)
    flat_weights = route_weights[0].reshape(tok_count * top_count)
    n_expert = lax.axis_size("expert")
    exp_dev = expert_gate.shape[1]
    expert_count = exp_dev * n_expert
    capacity = max(2, 2 * tok_count * top_count // expert_count)
    onehot = (flat_routes[:, None] == jnp.arange(expert_count, dtype=jnp.int32)[None, :]).astype(
        jnp.int32
    )
    ranked = jnp.sum((jnp.cumsum(onehot, axis=0) - 1) * onehot, axis=1)
    slot_index = flat_routes * capacity + ranked
    token_of = jnp.arange(tok_count * top_count, dtype=jnp.int32) // top_count
    outgoing = (
        jnp.zeros((expert_count * capacity, width), jnp.bfloat16)
        .at[slot_index]
        .set(rows_in[token_of])
    )
    outgoing = outgoing.reshape(n_expert, exp_dev, capacity, width)
    arrived = lax.all_to_all(outgoing, "expert", split_axis=0, concat_axis=2, tiled=True)
    slot_rows = arrived[0]
    gate_val = jnp.einsum(
        "esd,edf->esf", slot_rows, expert_gate[0], preferred_element_type=jnp.float32
    )
    up_val = jnp.einsum("esd,edf->esf", slot_rows, expert_up[0], preferred_element_type=jnp.float32)
    hidden = (jax.nn.silu(gate_val) * up_val).astype(jnp.bfloat16)
    expert_out = jnp.einsum(
        "esf,efd->esd", hidden, expert_down[0], preferred_element_type=jnp.float32
    ).astype(jnp.bfloat16)
    expert_out = expert_out.reshape(exp_dev, n_expert, capacity, width)
    came_back = lax.all_to_all(expert_out, "expert", split_axis=1, concat_axis=0, tiled=True)
    back_rows = came_back.reshape(expert_count * capacity, width)
    picked = back_rows[slot_index].astype(jnp.float32) * flat_weights[:, None]
    routed = jnp.sum(picked.reshape(tok_count, top_count, width), axis=1)
    layer_out = (rows_in.astype(jnp.float32) + routed).astype(jnp.bfloat16)
    handed = passed_along(layer_out, "section", 1)
    return (layer_out[None], handed[None])


OUTER = [(0, 1), (1, 0), (2, 3), (3, 2)]
INNER = [(1, 2), (2, 1)]


def on_line(tokens, routes, route_weights, expert_gate, expert_up, expert_down):
    rows = tokens[0]
    half = rows.shape[0] // 2
    first, second = rows[:half], rows[half:]
    me = lax.axis_index("expert")
    end = (me == 0) | (me == 3)

    def outer(value):
        return lax.ppermute(value, "expert", OUTER)

    def inner(value):
        return lax.ppermute(value, "expert", INNER)

    def pick(at_end, at_mid):
        return jnp.where(end, at_end, at_mid)

    def expert(block, weight):
        gate = jnp.dot(block, expert_gate[0, 0], preferred_element_type=jnp.float32)
        up = jnp.dot(block, expert_up[0, 0], preferred_element_type=jnp.float32)
        hidden = (jax.nn.silu(gate) * up).astype(jnp.bfloat16)
        out = jnp.dot(hidden, expert_down[0, 0], preferred_element_type=jnp.float32)
        return out.astype(jnp.bfloat16).astype(jnp.float32) * weight[:, None]

    def narrow(value):
        return value.astype(jnp.bfloat16)

    def wide(value):
        return value.astype(jnp.float32)

    names = jnp.arange(4, dtype=jnp.int32)[:, None, None]
    table = jnp.sum(
        jnp.where(routes[0].T[None] == names, route_weights[0].T[None], 0.0), axis=1
    )
    oa = outer(first)
    ia = inner(first)
    table_near = outer(table)
    table_mid = inner(jnp.stack([table, table_near]))
    table_far = outer(table_mid)
    weigh = lambda t: lax.dynamic_index_in_dim(t, me, 0, keepdims=False)
    w_own, w_near = weigh(table), weigh(table_near)
    w_two = weigh(pick(table_far[0], table_mid[0]))
    w_three = weigh(pick(table_far[1], table_mid[1]))
    lo, hi = slice(0, half), slice(half, None)

    total = wide(rows) + expert(rows, w_own)
    o1 = outer(pick(second, ia))
    i1 = inner(oa)
    p1 = expert(oa, w_near[lo])
    o2 = outer(pick(narrow(p1), i1))
    i2 = inner(o1)
    p2 = expert(pick(o1, ia), w_two[lo])
    o3 = outer(pick(narrow(p2), i2))
    i3 = inner(second)
    p3 = expert(pick(o2, i1), w_three[lo])
    o4 = outer(pick(narrow(p3), i3))
    i4 = inner(narrow(wide(o3) + p2))
    p4 = expert(pick(o3, i2), w_three[hi])
    o5 = outer(pick(narrow(p4), second))
    i5 = inner(narrow(wide(o4) + p3))
    p5 = expert(pick(o4, i3), w_two[hi])
    o6 = outer(pick(narrow(p5), narrow(wide(i5) + p1)))
    i6 = inner(narrow(wide(o5) + p4))
    p6 = expert(pick(o5, o1), w_near[hi])
    o7 = outer(pick(narrow(p6), narrow(wide(i6) + p6)))
    i7 = inner(narrow(wide(o6) + p5))
    out_lo = narrow(total[lo] + pick(wide(o6), wide(o2) + wide(i4)))
    next_lo = passed_along(out_lo, "section", 1)
    out_hi = narrow(total[hi] + wide(o7) + pick(0.0, wide(i7)))
    next_hi = passed_along(out_hi, "section", 1)
    layer_out = jnp.concatenate([out_lo, out_hi], axis=0)
    handed = jnp.concatenate([next_lo, next_hi], axis=0)
    return (layer_out[None], handed[None])


def solution(mesh):
    in_specs = (
        P("section", ("expert", "tensor"), None),
        P("section", ("expert", "tensor"), None),
        P("section", ("expert", "tensor"), None),
        P("section", "expert", None, None),
        P("section", "expert", None, None),
        P("section", "expert", None, None),
    )
    out_specs = (P("section", ("expert", "tensor"), None), P("section", ("expert", "tensor"), None))

    def per_device(*args):
        tokens, expert_gate = args[0], args[3]
        line = mesh.shape["expert"] == 4 and expert_gate.shape[1] == 1 and tokens.shape[1] % 32 == 0
        return (on_line if line else by_slots)(*args)

    return jax.shard_map(
        per_device, mesh=mesh, in_specs=in_specs, out_specs=out_specs, check_vma=False
    )
```

```python
import jax
import jax.numpy as jnp
from jax import lax
from jax.experimental import pallas as pl
from jax.experimental.pallas import tpu as pltpu
from jax.sharding import PartitionSpec as P


def passed_along(value, axis, steps):
    count = lax.axis_size(axis)
    leading, last = (max(0, -steps), min(count, count - steps))
    return lax.ppermute(value, axis, [(source, source + steps) for source in range(leading, last)])


def by_slots(tokens, routes, route_weights, expert_gate, expert_up, expert_down):
    rows_in = tokens[0]
    tok_count, width = rows_in.shape
    top_count = routes.shape[2]
    flat_routes = routes[0].reshape(tok_count * top_count)
    flat_weights = route_weights[0].reshape(tok_count * top_count)
    n_expert = lax.axis_size("expert")
    exp_dev = expert_gate.shape[1]
    expert_count = exp_dev * n_expert
    capacity = max(2, 2 * tok_count * top_count // expert_count)
    onehot = (flat_routes[:, None] == jnp.arange(expert_count, dtype=jnp.int32)[None, :]).astype(
        jnp.int32
    )
    ranked = jnp.sum((jnp.cumsum(onehot, axis=0) - 1) * onehot, axis=1)
    slot_index = flat_routes * capacity + ranked
    token_of = jnp.arange(tok_count * top_count, dtype=jnp.int32) // top_count
    outgoing = (
        jnp.zeros((expert_count * capacity, width), jnp.bfloat16)
        .at[slot_index]
        .set(rows_in[token_of])
    )
    outgoing = outgoing.reshape(n_expert, exp_dev, capacity, width)
    arrived = lax.all_to_all(outgoing, "expert", split_axis=0, concat_axis=2, tiled=True)
    slot_rows = arrived[0]
    gate_val = jnp.einsum(
        "esd,edf->esf", slot_rows, expert_gate[0], preferred_element_type=jnp.float32
    )
    up_val = jnp.einsum("esd,edf->esf", slot_rows, expert_up[0], preferred_element_type=jnp.float32)
    hidden = (jax.nn.silu(gate_val) * up_val).astype(jnp.bfloat16)
    expert_out = jnp.einsum(
        "esf,efd->esd", hidden, expert_down[0], preferred_element_type=jnp.float32
    ).astype(jnp.bfloat16)
    expert_out = expert_out.reshape(exp_dev, n_expert, capacity, width)
    came_back = lax.all_to_all(expert_out, "expert", split_axis=1, concat_axis=0, tiled=True)
    back_rows = came_back.reshape(expert_count * capacity, width)
    picked = back_rows[slot_index].astype(jnp.float32) * flat_weights[:, None]
    routed = jnp.sum(picked.reshape(tok_count, top_count, width), axis=1)
    layer_out = (rows_in.astype(jnp.float32) + routed).astype(jnp.bfloat16)
    handed = passed_along(layer_out, "section", 1)
    return (layer_out[None], handed[None])


OUTER = [(0, 1), (1, 0), (2, 3), (3, 2)]
INNER = [(1, 2), (2, 1)]
IN_VMEM = pl.BlockSpec(memory_space=pltpu.VMEM)
ANYWHERE = pl.BlockSpec(memory_space=pl.ANY)


def held(shape, dtype=jnp.bfloat16):
    return pltpu.VMEM(shape, dtype)


def wide(ref):
    return ref[...].astype(jnp.float32)


def narrow(value):
    return value.astype(jnp.bfloat16)


def position():
    me = lax.axis_index("expert")
    return me, (me == 0) | (me == 3)


def run(body, name, out_shape, *operands, scratch=(), specs=None, out_specs=None, work=(0, 0)):
    several = isinstance(out_shape, list)
    specs = specs or [IN_VMEM] * len(operands)
    operands = [
        pltpu.with_memory_space_constraint(x, pltpu.VMEM if s is IN_VMEM else pltpu.HBM)
        for x, s in zip(operands, specs)
    ]
    return pl.pallas_call(
        body,
        out_shape=out_shape,
        in_specs=specs,
        out_specs=out_specs or ([IN_VMEM] * len(out_shape) if several else IN_VMEM),
        scratch_shapes=list(scratch),
        compiler_params=pltpu.CompilerParams(vmem_limit_bytes=24 * 2**20),
        cost_estimate=pl.CostEstimate(flops=work[0], bytes_accessed=work[1], transcendentals=0),
        name=name,
    )(*operands)


def prepare(tokens, routes, weights, first, second, table, sems):
    half = first.shape[0]
    copies = [
        pltpu.make_async_copy(tokens.at[pl.ds(i * half, half)], part, sems.at[i])
        for i, part in enumerate((first, second))
    ]
    for copy in copies:
        copy.start()
    names = lax.broadcasted_iota(jnp.int32, table.shape, 0)
    total = jnp.zeros(table.shape, jnp.float32)
    for k in range(routes.shape[0]):
        total += jnp.where(routes[k : k + 1, :] == names, weights[k : k + 1, :], 0.0)
    table[...] = total
    for copy in copies:
        copy.wait()


def column(table, me, start, count):
    names = lax.broadcasted_iota(jnp.int32, table.shape, 0)
    row = jnp.sum(jnp.where(names == me, table, 0.0), axis=0, keepdims=True)[:, start : start + count]
    across = lax.broadcasted_iota(jnp.int32, (count, count), 1)
    down = lax.broadcasted_iota(jnp.int32, (count, count), 0)
    return jnp.sum(jnp.where(across == down, row, 0.0), axis=1, keepdims=True)


def expert_of(rows, gate_w, up_w, down_w):
    gate = jnp.dot(rows, gate_w[...], preferred_element_type=jnp.float32)
    up = jnp.dot(rows, up_w[...], preferred_element_type=jnp.float32)
    hidden = narrow(gate / (1.0 + jnp.exp(-gate)) * up)
    out = jnp.dot(hidden, down_w[...], preferred_element_type=jnp.float32)
    return narrow(out).astype(jnp.float32)


def own_pass(first, second, table, *refs):
    from_hbm, to_vmem, totals, sems = refs[0:3], refs[3:6], refs[6:8], refs[8]
    copies = [
        pltpu.make_async_copy(a, b, sems.at[i]) for i, (a, b) in enumerate(zip(from_hbm, to_vmem))
    ]
    for copy in copies:
        copy.start()
    me, _ = position()
    for copy in copies:
        copy.wait()
    half = first.shape[0]
    for i, part in enumerate((first, second)):
        out = expert_of(part[...], *to_vmem)
        totals[i][...] = wide(part) + out * column(table[...], me, i * half, half)


def pass_of(partner, late):
    def body(at_end, at_mid, table_a, table_b, table_c, gate_w, up_w, down_w, result):
        me, end = position()
        half = result.shape[0]
        if partner == 0:
            came = jnp.where(me % 2 == 0, 3, 1)
        elif partner == 1:
            came = jnp.where(me == 1, 3, jnp.where(me == 2, 1, 2))
        else:
            came = jnp.where(me == 0, 1, jnp.where(me == 3, 3, 2))
        table = jnp.where(came == 1, table_a[...], jnp.where(came == 2, table_b[...], table_c[...]))
        rows = jnp.where(end, at_end[...], at_mid[...])
        weight = column(table, me, half if late else 0, half)
        result[...] = narrow(expert_of(rows, gate_w, up_w, down_w) * weight)

    return body


def choose(at_end, at_mid, result):
    _, end = position()
    result[...] = jnp.where(end, at_end[...], at_mid[...])


def choose_sum(at_end, mid_a, mid_b, result):
    _, end = position()
    result[...] = jnp.where(end, at_end[...], narrow(wide(mid_a) + wide(mid_b)))


def add(a, b, result):
    result[...] = narrow(wide(a) + wide(b))


def finish_first(total, far, near, inner, result):
    _, end = position()
    result[...] = narrow(total[...] + jnp.where(end, wide(far), wide(near) + wide(inner)))


def finish_second(total, outer, inner, result):
    _, end = position()
    result[...] = narrow(total[...] + wide(outer) + jnp.where(end, 0.0, wide(inner)))


def join(first, second, whole, sems):
    half = first.shape[0]
    copies = [
        pltpu.make_async_copy(part, whole.at[pl.ds(i * half, half)], sems.at[i])
        for i, part in enumerate((first, second))
    ]
    for copy in copies:
        copy.start()
    for copy in copies:
        copy.wait()


def on_line(tokens, routes, route_weights, expert_gate, expert_up, expert_down):
    rows = tokens[0]
    count, width = rows.shape
    half = count // 2
    block = (half, width)
    weights = (expert_gate[0, 0], expert_up[0, 0], expert_down[0, 0])
    two_sems = [pltpu.SemaphoreType.DMA((2,))]

    def outer(value):
        return lax.ppermute(value, "expert", OUTER)

    def inner(value):
        return lax.ppermute(value, "expert", INNER)

    def turned(value, by):
        return lax.ppermute(value, "expert", [(s, (s + by) % 4) for s in range(4)])

    first, second, table = run(
        prepare,
        "prepare",
        [held(block), held(block), held((4, count), jnp.float32)],
        rows,
        routes[0].T,
        route_weights[0].T,
        scratch=two_sems,
        specs=[ANYWHERE, IN_VMEM, IN_VMEM],
    )
    o0, i0 = outer(first), inner(first)
    tables = [turned(table, by) for by in (1, 2, 3)]
    *weights, total_first, total_second = run(
        own_pass,
        "own_pass",
        [held(w.shape) for w in weights] + [held(block, jnp.float32)] * 2,
        first,
        second,
        table,
        *weights,
        scratch=[pltpu.SemaphoreType.DMA((3,))],
        specs=[IN_VMEM] * 3 + [ANYWHERE] * 3,
        work=(6 * count * weights[0].size, 6 * weights[0].size),
    )

    def expert(partner, late, at_end, at_mid):
        return run(
            pass_of(partner, late),
            "expert_pass",
            held(block),
            at_end,
            at_mid,
            *tables,
            *weights,
            work=(6 * half * weights[0].size, 6 * weights[0].size),
        )

    def mixed(body, *operands):
        return run(body, body.__name__, held(block), *operands)

    o1, i1 = outer(mixed(choose, second, i0)), inner(o0)
    p1 = expert(0, False, o0, o0)
    o2, i2 = outer(mixed(choose, p1, i1)), inner(o1)
    p2 = expert(1, False, o1, i0)
    o3, i3 = outer(mixed(choose, p2, i2)), inner(second)
    p3 = expert(2, False, o2, i1)
    o4, i4 = outer(mixed(choose, p3, i3)), inner(mixed(add, o3, p2))
    p4 = expert(2, True, o3, i2)
    o5, i5 = outer(mixed(choose, p4, second)), inner(mixed(add, o4, p3))
    p5 = expert(1, True, o4, i3)
    o6, i6 = outer(mixed(choose_sum, p5, i5, p1)), inner(mixed(add, o5, p4))
    p6 = expert(0, True, o5, o1)
    o7, i7 = outer(mixed(choose_sum, p6, i6, p6)), inner(mixed(add, o6, p5))
    out_first = mixed(finish_first, total_first, o6, o2, i4)
    next_first = passed_along(out_first, "section", 1)
    out_second = mixed(finish_second, total_second, o7, i7)
    next_second = passed_along(out_second, "section", 1)

    def joined(a, b):
        return run(
            join,
            "join",
            jax.ShapeDtypeStruct((count, width), jnp.bfloat16),
            a,
            b,
            scratch=two_sems,
            out_specs=ANYWHERE,
        )

    return (joined(out_first, out_second)[None], joined(next_first, next_second)[None])


def solution(mesh):
    in_specs = (
        P("section", ("expert", "tensor"), None),
        P("section", ("expert", "tensor"), None),
        P("section", ("expert", "tensor"), None),
        P("section", "expert", None, None),
        P("section", "expert", None, None),
        P("section", "expert", None, None),
    )
    out_specs = (P("section", ("expert", "tensor"), None), P("section", ("expert", "tensor"), None))

    def per_device(*args):
        tokens, expert_gate = args[0], args[3]
        line = mesh.shape["expert"] == 4 and expert_gate.shape[1] == 1 and tokens.shape[1] % 32 == 0
        return (on_line if line else by_slots)(*args)

    return jax.shard_map(
        per_device, mesh=mesh, in_specs=in_specs, out_specs=out_specs, check_vma=False
    )
```

```python
import jax
import jax.numpy as jnp
from jax import lax
from jax.experimental import pallas as pl
from jax.experimental.pallas import tpu as pltpu
from jax.sharding import PartitionSpec as P


def passed_along(value, axis, steps):
    count = lax.axis_size(axis)
    leading, last = (max(0, -steps), min(count, count - steps))
    return lax.ppermute(value, axis, [(source, source + steps) for source in range(leading, last)])


def by_slots(tokens, routes, route_weights, expert_gate, expert_up, expert_down):
    rows_in = tokens[0]
    tok_count, width = rows_in.shape
    top_count = routes.shape[2]
    flat_routes = routes[0].reshape(tok_count * top_count)
    flat_weights = route_weights[0].reshape(tok_count * top_count)
    n_expert = lax.axis_size("expert")
    exp_dev = expert_gate.shape[1]
    expert_count = exp_dev * n_expert
    capacity = max(2, 2 * tok_count * top_count // expert_count)
    onehot = (flat_routes[:, None] == jnp.arange(expert_count, dtype=jnp.int32)[None, :]).astype(
        jnp.int32
    )
    ranked = jnp.sum((jnp.cumsum(onehot, axis=0) - 1) * onehot, axis=1)
    slot_index = flat_routes * capacity + ranked
    token_of = jnp.arange(tok_count * top_count, dtype=jnp.int32) // top_count
    outgoing = (
        jnp.zeros((expert_count * capacity, width), jnp.bfloat16)
        .at[slot_index]
        .set(rows_in[token_of])
    )
    outgoing = outgoing.reshape(n_expert, exp_dev, capacity, width)
    arrived = lax.all_to_all(outgoing, "expert", split_axis=0, concat_axis=2, tiled=True)
    slot_rows = arrived[0]
    gate_val = jnp.einsum(
        "esd,edf->esf", slot_rows, expert_gate[0], preferred_element_type=jnp.float32
    )
    up_val = jnp.einsum("esd,edf->esf", slot_rows, expert_up[0], preferred_element_type=jnp.float32)
    hidden = (jax.nn.silu(gate_val) * up_val).astype(jnp.bfloat16)
    expert_out = jnp.einsum(
        "esf,efd->esd", hidden, expert_down[0], preferred_element_type=jnp.float32
    ).astype(jnp.bfloat16)
    expert_out = expert_out.reshape(exp_dev, n_expert, capacity, width)
    came_back = lax.all_to_all(expert_out, "expert", split_axis=1, concat_axis=0, tiled=True)
    back_rows = came_back.reshape(expert_count * capacity, width)
    picked = back_rows[slot_index].astype(jnp.float32) * flat_weights[:, None]
    routed = jnp.sum(picked.reshape(tok_count, top_count, width), axis=1)
    layer_out = (rows_in.astype(jnp.float32) + routed).astype(jnp.bfloat16)
    handed = passed_along(layer_out, "section", 1)
    return (layer_out[None], handed[None])


TAG = 128
IN_VMEM = pl.BlockSpec(memory_space=pltpu.VMEM)
ANYWHERE = pl.BlockSpec(memory_space=pl.ANY)


def held(shape, dtype=jnp.bfloat16):
    return pltpu.VMEM(shape, dtype)


def wide(ref):
    return ref[...].astype(jnp.float32)


def narrow(value):
    return value.astype(jnp.bfloat16)


def position():
    me = lax.axis_index("expert")
    return me, (me == 0) | (me == 3)


def run(body, name, out_shape, *operands, scratch=(), specs=None, out_specs=None, work=(0, 0)):
    several = isinstance(out_shape, list)
    specs = specs or [IN_VMEM] * len(operands)
    operands = [
        pltpu.with_memory_space_constraint(x, pltpu.VMEM if s is IN_VMEM else pltpu.HBM)
        for x, s in zip(operands, specs)
    ]
    return pl.pallas_call(
        body,
        out_shape=out_shape,
        in_specs=specs,
        out_specs=out_specs or ([IN_VMEM] * len(out_shape) if several else IN_VMEM),
        scratch_shapes=list(scratch),
        compiler_params=pltpu.CompilerParams(vmem_limit_bytes=24 * 2**20),
        cost_estimate=pl.CostEstimate(flops=work[0], bytes_accessed=work[1], transcendentals=0),
        name=name,
    )(*operands)


def prepare(tokens, routes, weights, first, second, routes_here, weights_here, sems):
    half, width = first.shape[0], tokens.shape[1]
    copies = [
        pltpu.make_async_copy(source, target, sems.at[i])
        for i, (source, target) in enumerate(
            (
                (routes, routes_here),
                (weights, weights_here),
                (tokens.at[pl.ds(0, half)], first.at[:, pl.ds(0, width)]),
                (tokens.at[pl.ds(half, half)], second),
            )
        )
    ]
    for copy in copies:
        copy.start()
    for copy in copies[:2]:
        copy.wait()
    names = lax.broadcasted_iota(jnp.int32, (8, 2 * half), 0)
    rest = jnp.zeros((8, 2 * half), jnp.float32)
    for k in range(routes.shape[0]):
        rest += jnp.where(routes_here[k : k + 1, :] == names, weights_here[k : k + 1, :], 0.0)
    pieces = []
    for _ in range(3):
        pieces.append(narrow(rest).astype(jnp.float32))
        rest = rest - pieces[-1]
    pieces += [pltpu.roll(piece, half, 1) for piece in pieces]
    pieces.append(jnp.zeros((TAG - 48, 2 * half), jnp.float32))
    tags = narrow(jnp.concatenate(pieces, axis=0).T[:half])
    for copy in copies[2:]:
        copy.wait()
    first[:, width:] = tags


def weight_of(tags, late):
    me, _ = position()
    lane = lax.broadcasted_iota(jnp.int32, tags.shape, 1)
    start = 24 if late else 0
    mine = (lane >= start) & (lane < start + 24) & (lane % 8 == me)
    return jnp.sum(jnp.where(mine, tags.astype(jnp.float32), 0.0), axis=1, keepdims=True)


def expert_of(rows, gate_w, up_w, down_w):
    gate = jnp.dot(rows, gate_w[...], preferred_element_type=jnp.float32)
    up = jnp.dot(rows, up_w[...], preferred_element_type=jnp.float32)
    hidden = narrow(gate / (1.0 + jnp.exp(-gate)) * up)
    out = jnp.dot(hidden, down_w[...], preferred_element_type=jnp.float32)
    return narrow(out).astype(jnp.float32)


def own_pass(first, second, gate_hbm, up_hbm, down_hbm, gate_w, up_w, down_w, total, sems):
    copies = [
        pltpu.make_async_copy(source, target, sems.at[i])
        for i, (source, target) in enumerate(
            ((gate_hbm, gate_w), (up_hbm, up_w), (down_hbm, down_w))
        )
    ]
    for copy in copies:
        copy.start()
    half, width = first.shape[0], total.shape[1]
    rows = jnp.concatenate([first[:, :width], second[...]], axis=0)
    tags = first[:, width:]
    weight = jnp.concatenate([weight_of(tags, False), weight_of(tags, True)], axis=0)
    copies[0].wait()
    gate = jnp.dot(rows, gate_w[...], preferred_element_type=jnp.float32)
    copies[1].wait()
    up = jnp.dot(rows, up_w[...], preferred_element_type=jnp.float32)
    hidden = narrow(gate / (1.0 + jnp.exp(-gate)) * up)
    copies[2].wait()
    out = jnp.dot(hidden, down_w[...], preferred_element_type=jnp.float32)
    total[...] = rows.astype(jnp.float32) + narrow(out).astype(jnp.float32) * weight


def pass_of(late):
    def body(at_end, at_mid, tag_end, tag_mid, gate_w, up_w, down_w, result):
        _, end = position()
        width = result.shape[1]
        rows = jnp.where(end, at_end[:, :width], at_mid[:, :width])
        weight = weight_of(jnp.where(end, tag_end[:, width:], tag_mid[:, width:]), late)
        result[...] = narrow(expert_of(rows, gate_w, up_w, down_w) * weight)

    return body


def choose(at_end, at_mid, result):
    _, end = position()
    width = min(at_end.shape[1], at_mid.shape[1], result.shape[1])
    result[:, :width] = jnp.where(end, at_end[:, :width], at_mid[:, :width])
    if result.shape[1] > width:
        wider, here = (at_mid, ~end) if at_mid.shape[1] > width else (at_end, end)
        rest = wider[:, width:]
        result[:, width:] = jnp.where(here, rest, jnp.zeros_like(rest))


def choose_sum(at_end, mid_a, mid_b, result):
    _, end = position()
    result[...] = jnp.where(end, at_end[...], narrow(wide(mid_a) + wide(mid_b)))


def add(a, b, result):
    result[...] = narrow(wide(a) + wide(b))


def finish_first(total, far, near, inner, result):
    _, end = position()
    half, width = result.shape
    at_mid = near[:, :width].astype(jnp.float32) + wide(inner)
    result[...] = narrow(total[:half] + jnp.where(end, wide(far), at_mid))


def finish_second(total, outer, inner, result):
    _, end = position()
    half = result.shape[0]
    result[...] = narrow(total[half:] + wide(outer) + jnp.where(end, 0.0, wide(inner)))


def join(first, second, whole, sems):
    half = first.shape[0]
    copies = [
        pltpu.make_async_copy(part, whole.at[pl.ds(i * half, half)], sems.at[i])
        for i, part in enumerate((first, second))
    ]
    for copy in copies:
        copy.start()
    for copy in copies:
        copy.wait()


def on_line(tokens, routes, route_weights, expert_gate, expert_up, expert_down):
    rows = tokens[0]
    count, width = rows.shape
    half = count // 2
    block = (half, width)
    weights = (expert_gate[0, 0], expert_up[0, 0], expert_down[0, 0])
    axes = ("section", "expert")
    sections = range(lax.axis_size("section"))
    outer_pairs = [(s * 4 + e, s * 4 + (e ^ 1)) for s in sections for e in range(4)]
    inner_pairs = [
        (s * 4 + e, s * 4 + 3 - e if e in (1, 2) else (s ^ 1) * 4 + e)
        for s in sections
        for e in range(4)
    ]

    def outer(value):
        return lax.ppermute(value, axes, outer_pairs)

    def inner(value):
        return lax.ppermute(value, axes, inner_pairs)

    tagged = (half, width + TAG)
    first, second = run(
        prepare,
        "prepare",
        [held(tagged), held(block)],
        rows,
        routes[0].T,
        route_weights[0].T,
        scratch=[
            held((routes.shape[2], count), jnp.int32),
            held((routes.shape[2], count), jnp.float32),
            pltpu.SemaphoreType.DMA((4,)),
        ],
        specs=[ANYWHERE] * 3,
    )
    o0, i0 = outer(first), inner(first)
    *weights, total = run(
        own_pass,
        "own_pass",
        [held(w.shape) for w in weights] + [held((count, width), jnp.float32)],
        first,
        second,
        *weights,
        scratch=[pltpu.SemaphoreType.DMA((3,))],
        specs=[IN_VMEM] * 2 + [ANYWHERE] * 3,
        work=(6 * count * weights[0].size, 6 * weights[0].size),
    )
    o0, i0, total, *weights = lax.optimization_barrier((o0, i0, total, *weights))

    def expert(late, rows, tags):
        return run(
            pass_of(late),
            "expert_pass",
            held(block),
            *rows,
            *tags,
            *weights,
            work=(6 * half * weights[0].size, 6 * weights[0].size),
        )

    def mixed(body, *operands, shape=block):
        return run(body, body.__name__, held(shape), *operands)

    near = (o0, o0)
    o1, i1 = outer(mixed(choose, second, i0, shape=tagged)), inner(o0)
    p1 = expert(False, near, near)
    o2, i2 = outer(mixed(choose, p1, i1, shape=tagged)), inner(o1)
    two = (o1, i0)
    p2 = expert(False, two, two)
    o3, i3 = outer(mixed(choose, p2, i2)), inner(second)
    three = (o2, i1)
    p3 = expert(False, three, three)
    o4, i4 = outer(mixed(choose, p3, i3)), inner(mixed(add, o3, p2))
    p4 = expert(True, (o3, i2), three)
    o5, i5 = outer(mixed(choose, p4, second)), inner(mixed(add, o4, p3))
    p5 = expert(True, (o4, i3), two)
    o6, i6 = outer(mixed(choose_sum, p5, i5, p1)), inner(mixed(add, o5, p4))
    p6 = expert(True, (o5, o1), near)
    o7, i7 = outer(mixed(choose_sum, p6, i6, p6)), inner(mixed(add, o6, p5))
    out_first = run(finish_first, "finish_first", held(block), total, o6, o2, i4)
    next_first = passed_along(out_first, "section", 1)
    out_second = run(finish_second, "finish_second", held(block), total, o7, i7)
    next_second = passed_along(out_second, "section", 1)

    def joined(a, b):
        return run(
            join,
            "join",
            jax.ShapeDtypeStruct((count, width), jnp.bfloat16),
            a,
            b,
            scratch=[pltpu.SemaphoreType.DMA((2,))],
            out_specs=ANYWHERE,
        )

    return (joined(out_first, out_second)[None], joined(next_first, next_second)[None])


def solution(mesh):
    in_specs = (
        P("section", ("expert", "tensor"), None),
        P("section", ("expert", "tensor"), None),
        P("section", ("expert", "tensor"), None),
        P("section", "expert", None, None),
        P("section", "expert", None, None),
        P("section", "expert", None, None),
    )
    out_specs = (P("section", ("expert", "tensor"), None), P("section", ("expert", "tensor"), None))

    def per_device(*args):
        tokens, expert_gate = args[0], args[3]
        line = mesh.shape["expert"] == 4 and mesh.shape["section"] % 2 == 0
        line = line and expert_gate.shape[1] == 1 and tokens.shape[1] == 128
        return (on_line if line else by_slots)(*args)

    return jax.shard_map(
        per_device, mesh=mesh, in_specs=in_specs, out_specs=out_specs, check_vma=False
    )
```

```python
import jax
import jax.numpy as jnp
from jax import lax
from jax.experimental import pallas as pl
from jax.experimental.pallas import tpu as pltpu
from jax.sharding import PartitionSpec as P


def passed_along(value, axis, steps):
    count = lax.axis_size(axis)
    leading, last = (max(0, -steps), min(count, count - steps))
    return lax.ppermute(value, axis, [(source, source + steps) for source in range(leading, last)])


def by_slots(tokens, routes, route_weights, expert_gate, expert_up, expert_down):
    rows_in = tokens[0]
    tok_count, width = rows_in.shape
    top_count = routes.shape[2]
    flat_routes = routes[0].reshape(tok_count * top_count)
    flat_weights = route_weights[0].reshape(tok_count * top_count)
    n_expert = lax.axis_size("expert")
    exp_dev = expert_gate.shape[1]
    expert_count = exp_dev * n_expert
    capacity = max(2, 2 * tok_count * top_count // expert_count)
    onehot = (flat_routes[:, None] == jnp.arange(expert_count, dtype=jnp.int32)[None, :]).astype(
        jnp.int32
    )
    ranked = jnp.sum((jnp.cumsum(onehot, axis=0) - 1) * onehot, axis=1)
    slot_index = flat_routes * capacity + ranked
    token_of = jnp.arange(tok_count * top_count, dtype=jnp.int32) // top_count
    outgoing = (
        jnp.zeros((expert_count * capacity, width), jnp.bfloat16)
        .at[slot_index]
        .set(rows_in[token_of])
    )
    outgoing = outgoing.reshape(n_expert, exp_dev, capacity, width)
    arrived = lax.all_to_all(outgoing, "expert", split_axis=0, concat_axis=2, tiled=True)
    slot_rows = arrived[0]
    gate_val = jnp.einsum(
        "esd,edf->esf", slot_rows, expert_gate[0], preferred_element_type=jnp.float32
    )
    up_val = jnp.einsum("esd,edf->esf", slot_rows, expert_up[0], preferred_element_type=jnp.float32)
    hidden = (jax.nn.silu(gate_val) * up_val).astype(jnp.bfloat16)
    expert_out = jnp.einsum(
        "esf,efd->esd", hidden, expert_down[0], preferred_element_type=jnp.float32
    ).astype(jnp.bfloat16)
    expert_out = expert_out.reshape(exp_dev, n_expert, capacity, width)
    came_back = lax.all_to_all(expert_out, "expert", split_axis=1, concat_axis=0, tiled=True)
    back_rows = came_back.reshape(expert_count * capacity, width)
    picked = back_rows[slot_index].astype(jnp.float32) * flat_weights[:, None]
    routed = jnp.sum(picked.reshape(tok_count, top_count, width), axis=1)
    layer_out = (rows_in.astype(jnp.float32) + routed).astype(jnp.bfloat16)
    handed = passed_along(layer_out, "section", 1)
    return (layer_out[None], handed[None])


TAG = 128
STREAMS = 2
IN_VMEM = pl.BlockSpec(memory_space=pltpu.VMEM)
ANYWHERE = pl.BlockSpec(memory_space=pl.ANY)


def held(shape, dtype=jnp.bfloat16):
    return pltpu.VMEM(shape, dtype)


def wide(ref):
    return ref[...].astype(jnp.float32)


def narrow(value):
    return value.astype(jnp.bfloat16)


def position():
    me = lax.axis_index("expert")
    return me, (me == 0) | (me == 3)


def run(body, name, out_shape, *operands, scratch=(), specs=None, out_specs=None, work=(0, 0)):
    several = isinstance(out_shape, list)
    specs = specs or [IN_VMEM] * len(operands)
    operands = [
        pltpu.with_memory_space_constraint(x, pltpu.VMEM if s is IN_VMEM else pltpu.HBM)
        for x, s in zip(operands, specs)
    ]
    return pl.pallas_call(
        body,
        out_shape=out_shape,
        in_specs=specs,
        out_specs=out_specs or ([IN_VMEM] * len(out_shape) if several else IN_VMEM),
        scratch_shapes=list(scratch),
        compiler_params=pltpu.CompilerParams(vmem_limit_bytes=24 * 2**20),
        cost_estimate=pl.CostEstimate(flops=work[0], bytes_accessed=work[1], transcendentals=0),
        name=name,
    )(*operands)


def prepare(tokens, routes, weights, *refs):
    pieces, (routes_here, weights_here, sems) = refs[: 2 * STREAMS], refs[2 * STREAMS :]
    (count, width), piece = tokens.shape, pieces[0].shape[0]
    moves = [(routes, routes_here), (weights, weights_here)] + [
        (tokens.at[pl.ds(i * piece, piece)], ref if i % 2 else ref.at[:, pl.ds(0, width)])
        for i, ref in enumerate(pieces)
    ]
    copies = [pltpu.make_async_copy(*move, sems.at[i]) for i, move in enumerate(moves)]
    for copy in copies:
        copy.start()
    for copy in copies[:2]:
        copy.wait()
    names = lax.broadcasted_iota(jnp.int32, (8, count), 0)
    rest = jnp.zeros((8, count), jnp.float32)
    for k in range(routes.shape[0]):
        rest += jnp.where(routes_here[k : k + 1, :] == names, weights_here[k : k + 1, :], 0.0)
    parts = []
    for _ in range(3):
        parts.append(narrow(rest).astype(jnp.float32))
        rest = rest - parts[-1]
    parts += [pltpu.roll(part, count - piece, 1) for part in parts]
    parts.append(jnp.zeros((TAG - 48, count), jnp.float32))
    tags = narrow(jnp.concatenate(parts, axis=0).T)
    for copy in copies[2:]:
        copy.wait()
    for s in range(STREAMS):
        pieces[2 * s][:, width:] = tags[2 * s * piece : (2 * s + 1) * piece]


def weight_of(tags, late):
    me, _ = position()
    lane = lax.broadcasted_iota(jnp.int32, tags.shape, 1)
    start = 24 if late else 0
    mine = (lane >= start) & (lane < start + 24) & (lane % 8 == me)
    return jnp.sum(jnp.where(mine, tags.astype(jnp.float32), 0.0), axis=1, keepdims=True)


def expert_of(rows, gate_w, up_w, down_w):
    gate = jnp.dot(rows, gate_w[...], preferred_element_type=jnp.float32)
    up = jnp.dot(rows, up_w[...], preferred_element_type=jnp.float32)
    hidden = narrow(gate / (1.0 + jnp.exp(-gate)) * up)
    out = jnp.dot(hidden, down_w[...], preferred_element_type=jnp.float32)
    return narrow(out).astype(jnp.float32)


def own_pass(*refs):
    pieces, refs = refs[: 2 * STREAMS], refs[2 * STREAMS :]
    from_hbm, (gate_w, up_w, down_w), total, sems = refs[:3], refs[3:6], refs[6], refs[7]
    copies = [
        pltpu.make_async_copy(source, target, sems.at[i])
        for i, (source, target) in enumerate(zip(from_hbm, (gate_w, up_w, down_w)))
    ]
    for copy in copies:
        copy.start()
    width = total.shape[1]
    rows = jnp.concatenate([piece[:, :width] for piece in pieces], axis=0)
    weight = jnp.concatenate(
        [weight_of(pieces[i // 2 * 2][:, width:], i % 2) for i in range(2 * STREAMS)], axis=0
    )
    copies[0].wait()
    gate = jnp.dot(rows, gate_w[...], preferred_element_type=jnp.float32)
    copies[1].wait()
    up = jnp.dot(rows, up_w[...], preferred_element_type=jnp.float32)
    hidden = narrow(gate / (1.0 + jnp.exp(-gate)) * up)
    copies[2].wait()
    out = jnp.dot(hidden, down_w[...], preferred_element_type=jnp.float32)
    total[...] = rows.astype(jnp.float32) + narrow(out).astype(jnp.float32) * weight


def pass_of(late):
    def body(*refs):
        _, end = position()
        given, (gate_w, up_w, down_w), results = refs[: -3 - STREAMS], refs[-3 - STREAMS : -STREAMS], refs[-STREAMS:]
        piece, width = results[0].shape
        rows, weight = [], []
        for s in range(STREAMS):
            at_end, at_mid, tag_end, tag_mid = given[4 * s : 4 * s + 4]
            rows.append(jnp.where(end, at_end[:, :width], at_mid[:, :width]))
            weight.append(weight_of(jnp.where(end, tag_end[:, width:], tag_mid[:, width:]), late))
        out = expert_of(jnp.concatenate(rows, axis=0), gate_w, up_w, down_w)
        out = narrow(out * jnp.concatenate(weight, axis=0))
        for s in range(STREAMS):
            results[s][...] = out[s * piece : (s + 1) * piece]

    return body


def choose(at_end, at_mid, result):
    _, end = position()
    width = min(at_end.shape[1], at_mid.shape[1], result.shape[1])
    result[:, :width] = jnp.where(end, at_end[:, :width], at_mid[:, :width])
    if result.shape[1] > width:
        wider, here = (at_mid, ~end) if at_mid.shape[1] > width else (at_end, end)
        rest = wider[:, width:]
        result[:, width:] = jnp.where(here, rest, jnp.zeros_like(rest))


def choose_sum(at_end, mid_a, mid_b, result):
    _, end = position()
    result[...] = jnp.where(end, at_end[...], narrow(wide(mid_a) + wide(mid_b)))


def add(a, b, result):
    result[...] = narrow(wide(a) + wide(b))


def finish_first(total, *refs):
    _, end = position()
    given, result = refs[:-1], refs[-1]
    (rows, width), piece = result.shape, result.shape[0] // STREAMS
    for s in range(STREAMS):
        far, near, inner = given[3 * s : 3 * s + 3]
        at_mid = near[:, :width].astype(jnp.float32) + wide(inner)
        own = total[2 * s * piece : (2 * s + 1) * piece]
        result[s * piece : (s + 1) * piece] = narrow(own + jnp.where(end, wide(far), at_mid))


def finish_second(stream):
    def body(total, outer, inner, result):
        _, end = position()
        piece = result.shape[0]
        own = total[(2 * stream + 1) * piece : (2 * stream + 2) * piece]
        result[...] = narrow(own + wide(outer) + jnp.where(end, 0.0, wide(inner)))

    return body


def join(firsts, *refs):
    seconds, whole, sems = refs[:STREAMS], refs[STREAMS], refs[STREAMS + 1]
    piece = seconds[0].shape[0]
    copies = []
    for s in range(STREAMS):
        for i, part in enumerate((firsts.at[pl.ds(s * piece, piece)], seconds[s])):
            place = 2 * s + i
            there = whole.at[pl.ds(place * piece, piece)]
            copies.append(pltpu.make_async_copy(part, there, sems.at[place]))
    for copy in copies:
        copy.start()
    for copy in copies:
        copy.wait()


def join_handed(*refs):
    @pl.when(lax.axis_index("section") == 0)
    def _():
        for ref in refs[: 1 + STREAMS]:
            ref[...] = jnp.zeros_like(ref)

    join(*refs)


def on_line(tokens, routes, route_weights, expert_gate, expert_up, expert_down):
    rows = tokens[0]
    count, width = rows.shape
    piece = count // (2 * STREAMS)
    block = (piece, width)
    both = range(STREAMS)
    weights = (expert_gate[0, 0], expert_up[0, 0], expert_down[0, 0])
    axes = ("section", "expert")
    sections = range(lax.axis_size("section"))
    outer_pairs = [(s * 4 + e, s * 4 + (e ^ 1)) for s in sections for e in range(4)]
    inner_pairs = [
        (s * 4 + e, s * 4 + 3 - e if e in (1, 2) else (s ^ 1) * 4 + e)
        for s in sections
        for e in range(4)
    ]

    def outer(value):
        return lax.ppermute(value, axes, outer_pairs)

    def inner(value):
        return lax.ppermute(value, axes, inner_pairs)

    tagged = (piece, width + TAG)
    pieces = run(
        prepare,
        "prepare",
        [held(tagged), held(block)] * STREAMS,
        rows,
        routes[0].T,
        route_weights[0].T,
        scratch=[
            held((routes.shape[2], count), jnp.int32),
            held((routes.shape[2], count), jnp.float32),
            pltpu.SemaphoreType.DMA((2 + 2 * STREAMS,)),
        ],
        specs=[ANYWHERE] * 3,
    )
    first, second = pieces[::2], pieces[1::2]
    o, i, p = [[None] * 8 for _ in both], [[None] * 8 for _ in both], [None] * 8

    def swap(k, s, to_outer, to_inner):
        o[s][k], i[s][k] = outer(to_outer), inner(to_inner)

    for s in both:
        swap(0, s, first[s], first[s])
    *weights, total = run(
        own_pass,
        "own_pass",
        [held(w.shape) for w in weights] + [held((count, width), jnp.float32)],
        *pieces,
        *weights,
        scratch=[pltpu.SemaphoreType.DMA((3,))],
        specs=[IN_VMEM] * len(pieces) + [ANYWHERE] * 3,
        work=(6 * count * weights[0].size, 6 * weights[0].size),
    )
    o[0][0], i[0][0], total, *weights = lax.optimization_barrier(
        (o[0][0], i[0][0], total, *weights)
    )

    def expert(late, given):
        return run(
            pass_of(late),
            "expert_pass",
            [held(block)] * STREAMS,
            *(x for s in both for x in given(s)),
            *weights,
            work=(6 * piece * STREAMS * weights[0].size, 6 * weights[0].size),
        )

    def mixed(body, *operands, shape=block):
        return run(body, body.__name__, held(shape), *operands)

    for s in both:
        swap(1, s, mixed(choose, second[s], i[s][0], shape=tagged), o[s][0])
    p[1] = expert(False, lambda s: (o[s][0],) * 4)
    for s in both:
        swap(2, s, mixed(choose, p[1][s], i[s][1], shape=tagged), o[s][1])
    p[2] = expert(False, lambda s: (o[s][1], i[s][0]) * 2)
    for s in both:
        swap(3, s, mixed(choose, p[2][s], i[s][2]), second[s])
    p[3] = expert(False, lambda s: (o[s][2], i[s][1]) * 2)
    for s in both:
        swap(4, s, mixed(choose, p[3][s], i[s][3]), mixed(add, o[s][3], p[2][s]))
    p[4] = expert(True, lambda s: (o[s][3], i[s][2], o[s][2], i[s][1]))
    for s in both:
        swap(5, s, mixed(choose, p[4][s], second[s]), mixed(add, o[s][4], p[3][s]))
    p[5] = expert(True, lambda s: (o[s][4], i[s][3], o[s][1], i[s][0]))
    for s in both:
        at_outer = mixed(choose_sum, p[5][s], i[s][5], p[1][s])
        swap(6, s, at_outer, mixed(add, o[s][5], p[4][s]))
    p[6] = expert(True, lambda s: (o[s][5], o[s][1], o[s][0], o[s][0]))
    for s in both:
        at_outer = mixed(choose_sum, p[6][s], i[s][6], p[6][s])
        swap(7, s, at_outer, mixed(add, o[s][6], p[5][s]))
    firsts = run(
        finish_first,
        "finish_first",
        held((STREAMS * piece, width)),
        total,
        *(x for s in both for x in (o[s][6], o[s][2], i[s][4])),
    )
    seconds = [
        run(finish_second(s), "finish_second", held(block), total, o[s][7], i[s][7]) for s in both
    ]

    def joined(body, parts):
        return run(
            body,
            body.__name__,
            jax.ShapeDtypeStruct((count, width), jnp.bfloat16),
            *parts,
            scratch=[pltpu.SemaphoreType.DMA((2 * STREAMS,))],
            out_specs=ANYWHERE,
        )

    parts = [firsts, *seconds]
    count_s = lax.axis_size("section")
    ring = [(s, (s + 1) % count_s) for s in range(count_s)]
    handed = [lax.ppermute(part, "section", ring) for part in parts]
    return (joined(join, parts)[None], joined(join_handed, handed)[None])


def solution(mesh):
    in_specs = (
        P("section", ("expert", "tensor"), None),
        P("section", ("expert", "tensor"), None),
        P("section", ("expert", "tensor"), None),
        P("section", "expert", None, None),
        P("section", "expert", None, None),
        P("section", "expert", None, None),
    )
    out_specs = (P("section", ("expert", "tensor"), None), P("section", ("expert", "tensor"), None))

    def per_device(*args):
        tokens, expert_gate = args[0], args[3]
        line = mesh.shape["expert"] == 4 and mesh.shape["section"] % 2 == 0
        line = line and expert_gate.shape[1] == 1 and tokens.shape[1] == 128
        return (on_line if line else by_slots)(*args)

    return jax.shard_map(
        per_device, mesh=mesh, in_specs=in_specs, out_specs=out_specs, check_vma=False
    )
```

```python
import jax
import jax.numpy as jnp
from jax import lax
from jax.experimental import pallas as pl
from jax.experimental.pallas import tpu as pltpu
from jax.sharding import PartitionSpec as P


def passed_along(value, axis, steps):
    count = lax.axis_size(axis)
    leading, last = (max(0, -steps), min(count, count - steps))
    return lax.ppermute(value, axis, [(source, source + steps) for source in range(leading, last)])


def by_slots(tokens, routes, route_weights, expert_gate, expert_up, expert_down):
    rows_in = tokens[0]
    tok_count, width = rows_in.shape
    top_count = routes.shape[2]
    flat_routes = routes[0].reshape(tok_count * top_count)
    flat_weights = route_weights[0].reshape(tok_count * top_count)
    n_expert = lax.axis_size("expert")
    exp_dev = expert_gate.shape[1]
    expert_count = exp_dev * n_expert
    capacity = max(2, 2 * tok_count * top_count // expert_count)
    onehot = (flat_routes[:, None] == jnp.arange(expert_count, dtype=jnp.int32)[None, :]).astype(
        jnp.int32
    )
    ranked = jnp.sum((jnp.cumsum(onehot, axis=0) - 1) * onehot, axis=1)
    slot_index = flat_routes * capacity + ranked
    token_of = jnp.arange(tok_count * top_count, dtype=jnp.int32) // top_count
    outgoing = (
        jnp.zeros((expert_count * capacity, width), jnp.bfloat16)
        .at[slot_index]
        .set(rows_in[token_of])
    )
    outgoing = outgoing.reshape(n_expert, exp_dev, capacity, width)
    arrived = lax.all_to_all(outgoing, "expert", split_axis=0, concat_axis=2, tiled=True)
    slot_rows = arrived[0]
    gate_val = jnp.einsum(
        "esd,edf->esf", slot_rows, expert_gate[0], preferred_element_type=jnp.float32
    )
    up_val = jnp.einsum("esd,edf->esf", slot_rows, expert_up[0], preferred_element_type=jnp.float32)
    hidden = (jax.nn.silu(gate_val) * up_val).astype(jnp.bfloat16)
    expert_out = jnp.einsum(
        "esf,efd->esd", hidden, expert_down[0], preferred_element_type=jnp.float32
    ).astype(jnp.bfloat16)
    expert_out = expert_out.reshape(exp_dev, n_expert, capacity, width)
    came_back = lax.all_to_all(expert_out, "expert", split_axis=1, concat_axis=0, tiled=True)
    back_rows = came_back.reshape(expert_count * capacity, width)
    picked = back_rows[slot_index].astype(jnp.float32) * flat_weights[:, None]
    routed = jnp.sum(picked.reshape(tok_count, top_count, width), axis=1)
    layer_out = (rows_in.astype(jnp.float32) + routed).astype(jnp.bfloat16)
    handed = passed_along(layer_out, "section", 1)
    return (layer_out[None], handed[None])


TAG = 128
STREAMS = 2
IN_VMEM = pl.BlockSpec(memory_space=pltpu.VMEM)
ANYWHERE = pl.BlockSpec(memory_space=pl.ANY)


def held(shape, dtype=jnp.bfloat16):
    return pltpu.VMEM(shape, dtype)


def wide(ref):
    return ref[...].astype(jnp.float32)


def narrow(value):
    return value.astype(jnp.bfloat16)


def position():
    me = lax.axis_index("expert")
    return me, (me == 0) | (me == 3)


def run(body, name, out_shape, *operands, scratch=(), specs=None, out_specs=None, work=(0, 0)):
    several = isinstance(out_shape, list)
    specs = specs or [IN_VMEM] * len(operands)
    operands = [
        pltpu.with_memory_space_constraint(x, pltpu.VMEM if s is IN_VMEM else pltpu.HBM)
        for x, s in zip(operands, specs)
    ]
    return pl.pallas_call(
        body,
        out_shape=out_shape,
        in_specs=specs,
        out_specs=out_specs or ([IN_VMEM] * len(out_shape) if several else IN_VMEM),
        scratch_shapes=list(scratch),
        compiler_params=pltpu.CompilerParams(vmem_limit_bytes=24 * 2**20),
        cost_estimate=pl.CostEstimate(flops=work[0], bytes_accessed=work[1], transcendentals=0),
        name=name,
    )(*operands)


def prepare(tokens, routes, weights, *refs):
    pieces, (routes_here, weights_here, sems) = refs[: 2 * STREAMS], refs[2 * STREAMS :]
    (count, width), piece = tokens.shape, pieces[0].shape[0]
    moves = [(routes, routes_here), (weights, weights_here)] + [
        (tokens.at[pl.ds(i * piece, piece)], ref if i % 2 else ref.at[:, pl.ds(0, width)])
        for i, ref in enumerate(pieces)
    ]
    copies = [pltpu.make_async_copy(*move, sems.at[i]) for i, move in enumerate(moves)]
    for copy in copies:
        copy.start()
    for copy in copies[:2]:
        copy.wait()
    names = lax.broadcasted_iota(jnp.int32, (8, count), 0)
    rest = jnp.zeros((8, count), jnp.float32)
    for k in range(routes.shape[0]):
        rest += jnp.where(routes_here[k : k + 1, :] == names, weights_here[k : k + 1, :], 0.0)
    parts = []
    for _ in range(3):
        parts.append(narrow(rest).astype(jnp.float32))
        rest = rest - parts[-1]
    parts += [pltpu.roll(part, count - piece, 1) for part in parts]
    parts.append(jnp.zeros((TAG - 48, count), jnp.float32))
    tags = narrow(jnp.concatenate(parts, axis=0).T)
    for copy in copies[2:]:
        copy.wait()
    for s in range(STREAMS):
        pieces[2 * s][:, width:] = tags[2 * s * piece : (2 * s + 1) * piece]


def weight_of(tags, late):
    me, _ = position()
    lane = lax.broadcasted_iota(jnp.int32, tags.shape, 1)
    start = 24 if late else 0
    mine = (lane >= start) & (lane < start + 24) & (lane % 8 == me)
    return jnp.sum(jnp.where(mine, tags.astype(jnp.float32), 0.0), axis=1, keepdims=True)


def expert_of(rows, gate_w, up_w, down_w):
    gate = jnp.dot(rows, gate_w[...], preferred_element_type=jnp.float32)
    up = jnp.dot(rows, up_w[...], preferred_element_type=jnp.float32)
    hidden = narrow(gate / (1.0 + jnp.exp(-gate)) * up)
    out = jnp.dot(hidden, down_w[...], preferred_element_type=jnp.float32)
    return narrow(out).astype(jnp.float32)


def own_pass(*refs):
    pieces, (gate_w, up_w, down_w, total) = refs[: 2 * STREAMS], refs[2 * STREAMS :]
    width = total.shape[1]
    rows = jnp.concatenate([piece[:, :width] for piece in pieces], axis=0)
    weight = jnp.concatenate(
        [weight_of(pieces[i // 2 * 2][:, width:], i % 2) for i in range(2 * STREAMS)], axis=0
    )
    total[...] = rows.astype(jnp.float32) + expert_of(rows, gate_w, up_w, down_w) * weight


def load(*refs):
    sems = refs[6]
    copies = [pltpu.make_async_copy(refs[i], refs[3 + i], sems.at[i]) for i in range(3)]
    for copy in copies:
        copy.start()
    for copy in copies:
        copy.wait()


def pass_of(late):
    def body(*refs):
        _, end = position()
        given, (gate_w, up_w, down_w), results = refs[: -3 - STREAMS], refs[-3 - STREAMS : -STREAMS], refs[-STREAMS:]
        piece, width = results[0].shape
        rows, weight = [], []
        for s in range(STREAMS):
            at_end, at_mid, tag_end, tag_mid = given[4 * s : 4 * s + 4]
            rows.append(jnp.where(end, at_end[:, :width], at_mid[:, :width]))
            weight.append(weight_of(jnp.where(end, tag_end[:, width:], tag_mid[:, width:]), late))
        out = expert_of(jnp.concatenate(rows, axis=0), gate_w, up_w, down_w)
        out = narrow(out * jnp.concatenate(weight, axis=0))
        for s in range(STREAMS):
            results[s][...] = out[s * piece : (s + 1) * piece]

    return body


def choose(at_end, at_mid, result):
    _, end = position()
    width = min(at_end.shape[1], at_mid.shape[1], result.shape[1])
    result[:, :width] = jnp.where(end, at_end[:, :width], at_mid[:, :width])
    if result.shape[1] > width:
        wider, here = (at_mid, ~end) if at_mid.shape[1] > width else (at_end, end)
        rest = wider[:, width:]
        result[:, width:] = jnp.where(here, rest, jnp.zeros_like(rest))


def choose_sum(at_end, mid_a, mid_b, result):
    _, end = position()
    result[...] = jnp.where(end, at_end[...], narrow(wide(mid_a) + wide(mid_b)))


def add(a, b, result):
    result[...] = narrow(wide(a) + wide(b))


def finish_first(total, *refs):
    _, end = position()
    given, result = refs[:-1], refs[-1]
    (rows, width), piece = result.shape, result.shape[0] // STREAMS
    for s in range(STREAMS):
        far, near, inner = given[3 * s : 3 * s + 3]
        at_mid = near[:, :width].astype(jnp.float32) + wide(inner)
        own = total[2 * s * piece : (2 * s + 1) * piece]
        result[s * piece : (s + 1) * piece] = narrow(own + jnp.where(end, wide(far), at_mid))


def finish_second(stream):
    def body(total, outer, inner, result):
        _, end = position()
        piece = result.shape[0]
        own = total[(2 * stream + 1) * piece : (2 * stream + 2) * piece]
        result[...] = narrow(own + wide(outer) + jnp.where(end, 0.0, wide(inner)))

    return body


def join(firsts, *refs):
    seconds, whole, sems = refs[:STREAMS], refs[STREAMS], refs[STREAMS + 1]
    piece = seconds[0].shape[0]
    copies = []
    for s in range(STREAMS):
        for i, part in enumerate((firsts.at[pl.ds(s * piece, piece)], seconds[s])):
            place = 2 * s + i
            there = whole.at[pl.ds(place * piece, piece)]
            copies.append(pltpu.make_async_copy(part, there, sems.at[place]))
    for copy in copies:
        copy.start()
    for copy in copies:
        copy.wait()


def join_handed(*refs):
    @pl.when(lax.axis_index("section") == 0)
    def _():
        for ref in refs[: 1 + STREAMS]:
            ref[...] = jnp.zeros_like(ref)

    join(*refs)


def on_line(tokens, routes, route_weights, expert_gate, expert_up, expert_down):
    rows = tokens[0]
    count, width = rows.shape
    piece = count // (2 * STREAMS)
    block = (piece, width)
    both = range(STREAMS)
    weights = (expert_gate[0, 0], expert_up[0, 0], expert_down[0, 0])
    axes = ("section", "expert")
    sections = range(lax.axis_size("section"))
    outer_pairs = [(s * 4 + e, s * 4 + (e ^ 1)) for s in sections for e in range(4)]
    inner_pairs = [
        (s * 4 + e, s * 4 + 3 - e if e in (1, 2) else (s ^ 1) * 4 + e)
        for s in sections
        for e in range(4)
    ]

    def outer(value):
        return lax.ppermute(value, axes, outer_pairs)

    def inner(value):
        return lax.ppermute(value, axes, inner_pairs)

    tagged = (piece, width + TAG)
    pieces = run(
        prepare,
        "prepare",
        [held(tagged), held(block)] * STREAMS,
        rows,
        routes[0].T,
        route_weights[0].T,
        scratch=[
            held((routes.shape[2], count), jnp.int32),
            held((routes.shape[2], count), jnp.float32),
            pltpu.SemaphoreType.DMA((2 + 2 * STREAMS,)),
        ],
        specs=[ANYWHERE] * 3,
    )
    first, second = pieces[::2], pieces[1::2]
    o, i, p = [[None] * 8 for _ in both], [[None] * 8 for _ in both], [None] * 8

    def swap(k, s, to_outer, to_inner):
        if 5 <= k <= 7:
            i[s][k - 1], to_inner = lax.optimization_barrier((i[s][k - 1], to_inner))
        o[s][k], i[s][k] = outer(to_outer), inner(to_inner)

    for s in both:
        swap(0, s, first[s], first[s])
    weights = run(
        load,
        "load",
        [held(w.shape) for w in weights],
        *weights,
        scratch=[pltpu.SemaphoreType.DMA((3,))],
        specs=[ANYWHERE] * 3,
        work=(0, 6 * weights[0].size),
    )
    i[0][0], *weights = lax.optimization_barrier((i[0][0], *weights))

    def expert(late, given):
        return run(
            pass_of(late),
            "expert_pass",
            [held(block)] * STREAMS,
            *(x for s in both for x in given(s)),
            *weights,
            work=(6 * piece * STREAMS * weights[0].size, 6 * weights[0].size),
        )

    def mixed(body, *operands, shape=block):
        return run(body, body.__name__, held(shape), *operands)

    for s in both:
        swap(1, s, mixed(choose, second[s], i[s][0], shape=tagged), o[s][0])
    p[1] = expert(False, lambda s: (o[s][0],) * 4)
    for s in both:
        swap(2, s, mixed(choose, p[1][s], i[s][1], shape=tagged), o[s][1])
    p[2] = expert(False, lambda s: (o[s][1], i[s][0]) * 2)
    total = run(
        own_pass,
        "own_pass",
        held((count, width), jnp.float32),
        *pieces,
        *weights,
        work=(6 * count * weights[0].size, 6 * weights[0].size),
    )
    o[0][2], i[0][2], total = lax.optimization_barrier((o[0][2], i[0][2], total))
    for s in both:
        swap(3, s, mixed(choose, p[2][s], i[s][2]), second[s])
    p[3] = expert(False, lambda s: (o[s][2], i[s][1]) * 2)
    for s in both:
        swap(4, s, mixed(choose, p[3][s], i[s][3]), mixed(add, o[s][3], p[2][s]))
    p[4] = expert(True, lambda s: (o[s][3], i[s][2], o[s][2], i[s][1]))
    for s in both:
        swap(5, s, mixed(choose, p[4][s], second[s]), mixed(add, o[s][4], p[3][s]))
    p[5] = expert(True, lambda s: (o[s][4], i[s][3], o[s][1], i[s][0]))
    for s in both:
        at_outer = mixed(choose_sum, p[5][s], i[s][5], p[1][s])
        swap(6, s, at_outer, mixed(add, o[s][5], p[4][s]))
    p[6] = expert(True, lambda s: (o[s][5], o[s][1], o[s][0], o[s][0]))
    for s in both:
        at_outer = mixed(choose_sum, p[6][s], i[s][6], p[6][s])
        swap(7, s, at_outer, mixed(add, o[s][6], p[5][s]))
    firsts = run(
        finish_first,
        "finish_first",
        held((STREAMS * piece, width)),
        total,
        *(x for s in both for x in (o[s][6], o[s][2], i[s][4])),
    )
    seconds = [
        run(finish_second(s), "finish_second", held(block), total, o[s][7], i[s][7]) for s in both
    ]

    def joined(body, parts):
        return run(
            body,
            body.__name__,
            jax.ShapeDtypeStruct((count, width), jnp.bfloat16),
            *parts,
            scratch=[pltpu.SemaphoreType.DMA((2 * STREAMS,))],
            out_specs=ANYWHERE,
        )

    parts = [firsts, *seconds]
    count_s = lax.axis_size("section")
    ring = [(s, (s + 1) % count_s) for s in range(count_s)]
    handed = [lax.ppermute(part, "section", ring) for part in parts]
    return (joined(join, parts)[None], joined(join_handed, handed)[None])


def solution(mesh):
    in_specs = (
        P("section", ("expert", "tensor"), None),
        P("section", ("expert", "tensor"), None),
        P("section", ("expert", "tensor"), None),
        P("section", "expert", None, None),
        P("section", "expert", None, None),
        P("section", "expert", None, None),
    )
    out_specs = (P("section", ("expert", "tensor"), None), P("section", ("expert", "tensor"), None))

    def per_device(*args):
        tokens, expert_gate = args[0], args[3]
        line = mesh.shape["expert"] == 4 and mesh.shape["section"] % 2 == 0
        line = line and expert_gate.shape[1] == 1 and tokens.shape[1] == 128
        return (on_line if line else by_slots)(*args)

    return jax.shard_map(
        per_device, mesh=mesh, in_specs=in_specs, out_specs=out_specs, check_vma=False
    )
```

```python
import jax
import jax.numpy as jnp
from jax import lax
from jax.experimental import pallas as pl
from jax.experimental.pallas import tpu as pltpu
from jax.sharding import PartitionSpec as P


def passed_along(value, axis, steps):
    count = lax.axis_size(axis)
    leading, last = (max(0, -steps), min(count, count - steps))
    return lax.ppermute(value, axis, [(source, source + steps) for source in range(leading, last)])


def by_slots(tokens, routes, route_weights, expert_gate, expert_up, expert_down):
    rows_in = tokens[0]
    tok_count, width = rows_in.shape
    top_count = routes.shape[2]
    flat_routes = routes[0].reshape(tok_count * top_count)
    flat_weights = route_weights[0].reshape(tok_count * top_count)
    n_expert = lax.axis_size("expert")
    exp_dev = expert_gate.shape[1]
    expert_count = exp_dev * n_expert
    capacity = max(2, 2 * tok_count * top_count // expert_count)
    onehot = (flat_routes[:, None] == jnp.arange(expert_count, dtype=jnp.int32)[None, :]).astype(
        jnp.int32
    )
    ranked = jnp.sum((jnp.cumsum(onehot, axis=0) - 1) * onehot, axis=1)
    slot_index = flat_routes * capacity + ranked
    token_of = jnp.arange(tok_count * top_count, dtype=jnp.int32) // top_count
    outgoing = (
        jnp.zeros((expert_count * capacity, width), jnp.bfloat16)
        .at[slot_index]
        .set(rows_in[token_of])
    )
    outgoing = outgoing.reshape(n_expert, exp_dev, capacity, width)
    arrived = lax.all_to_all(outgoing, "expert", split_axis=0, concat_axis=2, tiled=True)
    slot_rows = arrived[0]
    gate_val = jnp.einsum(
        "esd,edf->esf", slot_rows, expert_gate[0], preferred_element_type=jnp.float32
    )
    up_val = jnp.einsum("esd,edf->esf", slot_rows, expert_up[0], preferred_element_type=jnp.float32)
    hidden = (jax.nn.silu(gate_val) * up_val).astype(jnp.bfloat16)
    expert_out = jnp.einsum(
        "esf,efd->esd", hidden, expert_down[0], preferred_element_type=jnp.float32
    ).astype(jnp.bfloat16)
    expert_out = expert_out.reshape(exp_dev, n_expert, capacity, width)
    came_back = lax.all_to_all(expert_out, "expert", split_axis=1, concat_axis=0, tiled=True)
    back_rows = came_back.reshape(expert_count * capacity, width)
    picked = back_rows[slot_index].astype(jnp.float32) * flat_weights[:, None]
    routed = jnp.sum(picked.reshape(tok_count, top_count, width), axis=1)
    layer_out = (rows_in.astype(jnp.float32) + routed).astype(jnp.bfloat16)
    handed = passed_along(layer_out, "section", 1)
    return (layer_out[None], handed[None])


TAG = 128
STREAMS = 2
IN_VMEM = pl.BlockSpec(memory_space=pltpu.VMEM)
ANYWHERE = pl.BlockSpec(memory_space=pl.ANY)


def held(shape, dtype=jnp.bfloat16):
    return pltpu.VMEM(shape, dtype)


def wide(ref):
    return ref[...].astype(jnp.float32)


def narrow(value):
    return value.astype(jnp.bfloat16)


def position():
    me = lax.axis_index("expert")
    return me, (me == 0) | (me == 3)


def run(body, name, out_shape, *operands, scratch=(), specs=None, out_specs=None, work=(0, 0)):
    several = isinstance(out_shape, list)
    specs = specs or [IN_VMEM] * len(operands)
    operands = [
        pltpu.with_memory_space_constraint(x, pltpu.VMEM if s is IN_VMEM else pltpu.HBM)
        for x, s in zip(operands, specs)
    ]
    return pl.pallas_call(
        body,
        out_shape=out_shape,
        in_specs=specs,
        out_specs=out_specs or ([IN_VMEM] * len(out_shape) if several else IN_VMEM),
        scratch_shapes=list(scratch),
        compiler_params=pltpu.CompilerParams(vmem_limit_bytes=24 * 2**20),
        cost_estimate=pl.CostEstimate(flops=work[0], bytes_accessed=work[1], transcendentals=0),
        name=name,
    )(*operands)


def prepare(tokens, routes, weights, *refs):
    pieces, (routes_here, weights_here, sems) = refs[: 2 * STREAMS], refs[2 * STREAMS :]
    (count, width), piece = tokens.shape, pieces[0].shape[0]
    moves = [(routes, routes_here), (weights, weights_here)] + [
        (tokens.at[pl.ds(i * piece, piece)], ref if i % 2 else ref.at[:, pl.ds(0, width)])
        for i, ref in enumerate(pieces)
    ]
    copies = [pltpu.make_async_copy(*move, sems.at[i]) for i, move in enumerate(moves)]
    for copy in copies:
        copy.start()
    for copy in copies[:2]:
        copy.wait()
    names = lax.broadcasted_iota(jnp.int32, (8, count), 0)
    rest = jnp.zeros((8, count), jnp.float32)
    for k in range(routes.shape[0]):
        rest += jnp.where(routes_here[k : k + 1, :] == names, weights_here[k : k + 1, :], 0.0)
    parts = []
    for _ in range(3):
        parts.append(narrow(rest).astype(jnp.float32))
        rest = rest - parts[-1]
    parts += [pltpu.roll(part, count - piece, 1) for part in parts]
    parts.append(jnp.zeros((TAG - 48, count), jnp.float32))
    tags = narrow(jnp.concatenate(parts, axis=0).T)
    for copy in copies[2:]:
        copy.wait()
    for s in range(STREAMS):
        pieces[2 * s][:, width:] = tags[2 * s * piece : (2 * s + 1) * piece]


def weight_of(tags, late):
    me, _ = position()
    lane = lax.broadcasted_iota(jnp.int32, tags.shape, 1)
    start = 24 if late else 0
    mine = (lane >= start) & (lane < start + 24) & (lane % 8 == me)
    return jnp.sum(jnp.where(mine, tags.astype(jnp.float32), 0.0), axis=1, keepdims=True)


def expert_of(rows, gate_w, up_w, down_w):
    gate = jnp.dot(rows, gate_w[...], preferred_element_type=jnp.float32)
    up = jnp.dot(rows, up_w[...], preferred_element_type=jnp.float32)
    hidden = narrow(gate / (1.0 + jnp.exp(-gate)) * up)
    out = jnp.dot(hidden, down_w[...], preferred_element_type=jnp.float32)
    return narrow(out).astype(jnp.float32)


def load(*refs):
    sems = refs[6]
    copies = [pltpu.make_async_copy(refs[i], refs[3 + i], sems.at[i]) for i in range(3)]
    for copy in copies:
        copy.start()
    for copy in copies:
        copy.wait()


def pass_of(late):
    def body(*refs):
        _, end = position()
        given, refs = refs[: 4 * STREAMS], refs[4 * STREAMS :]
        pieces = refs[: 2 * STREAMS] if len(refs) > 3 + STREAMS else ()
        refs = refs[len(pieces) :]
        weights, results, totals = refs[:3], refs[3 : 3 + STREAMS], refs[3 + STREAMS :]
        piece, width = results[0].shape
        rows, weight = [], []
        for s in range(STREAMS):
            at_end, at_mid, tag_end, tag_mid = given[4 * s : 4 * s + 4]
            rows.append(jnp.where(end, at_end[:, :width], at_mid[:, :width]))
            weight.append(weight_of(jnp.where(end, tag_end[:, width:], tag_mid[:, width:]), late))
        for i, ref in enumerate(pieces):
            rows.append(ref[:, :width])
            weight.append(weight_of(pieces[i // 2 * 2][:, width:], i % 2))
        rows, weight = jnp.concatenate(rows, axis=0), jnp.concatenate(weight, axis=0)
        out = expert_of(rows, *weights) * weight
        for s in range(STREAMS):
            results[s][...] = narrow(out[s * piece : (s + 1) * piece])
        for total in totals:
            start = STREAMS * piece
            total[...] = rows[start:].astype(jnp.float32) + out[start:]

    return body


def choose(at_end, at_mid, result):
    _, end = position()
    width = min(at_end.shape[1], at_mid.shape[1], result.shape[1])
    result[:, :width] = jnp.where(end, at_end[:, :width], at_mid[:, :width])
    if result.shape[1] > width:
        wider, here = (at_mid, ~end) if at_mid.shape[1] > width else (at_end, end)
        rest = wider[:, width:]
        result[:, width:] = jnp.where(here, rest, jnp.zeros_like(rest))


def choose_sum(at_end, mid_a, mid_b, result):
    _, end = position()
    result[...] = jnp.where(end, at_end[...], narrow(wide(mid_a) + wide(mid_b)))


def add(a, b, result):
    result[...] = narrow(wide(a) + wide(b))


def finish_first(stream):
    def body(total, far, near, inner, result):
        _, end = position()
        piece, width = result.shape
        own = total[2 * stream * piece : (2 * stream + 1) * piece]
        at_mid = near[:, :width].astype(jnp.float32) + wide(inner)
        result[...] = narrow(own + jnp.where(end, wide(far), at_mid))

    return body


def finish_second(stream):
    def body(total, outer, inner, result):
        _, end = position()
        piece = result.shape[0]
        own = total[(2 * stream + 1) * piece : (2 * stream + 2) * piece]
        result[...] = narrow(own + wide(outer) + jnp.where(end, 0.0, wide(inner)))

    return body


def join(*refs):
    parts, whole, sems = refs[:-2], refs[-2], refs[-1]
    copies, row = [], 0
    for i, part in enumerate(parts):
        there = whole.at[pl.ds(row, part.shape[0])]
        copies.append(pltpu.make_async_copy(part, there, sems.at[i]))
        row += part.shape[0]
    for copy in copies:
        copy.start()
    for copy in copies:
        copy.wait()


def join_two(a, b, result):
    half = a.shape[0]
    result[:half] = a[...]
    result[half:] = b[...]


def join_apart(firsts, *refs):
    half = firsts.shape[0] // 2
    join_handed(firsts.at[:half], refs[0], firsts.at[half:], *refs[1:])


def join_handed(*refs):
    @pl.when(lax.axis_index("section") == 0)
    def _():
        for ref in refs[:-2]:
            ref[...] = jnp.zeros_like(ref)

    join(*refs)


def on_line(tokens, routes, route_weights, expert_gate, expert_up, expert_down):
    rows = tokens[0]
    count, width = rows.shape
    piece = count // (2 * STREAMS)
    block = (piece, width)
    both = range(STREAMS)
    weights = (expert_gate[0, 0], expert_up[0, 0], expert_down[0, 0])
    axes = ("section", "expert")
    sections = range(lax.axis_size("section"))
    outer_pairs = [(s * 4 + e, s * 4 + (e ^ 1)) for s in sections for e in range(4)]
    inner_pairs = [
        (s * 4 + e, s * 4 + 3 - e if e in (1, 2) else (s ^ 1) * 4 + e)
        for s in sections
        for e in range(4)
    ]

    def outer(value):
        return lax.ppermute(value, axes, outer_pairs)

    def inner(value):
        return lax.ppermute(value, axes, inner_pairs)

    tagged = (piece, width + TAG)
    pieces = run(
        prepare,
        "prepare",
        [held(tagged), held(block)] * STREAMS,
        rows,
        routes[0].T,
        route_weights[0].T,
        scratch=[
            held((routes.shape[2], count), jnp.int32),
            held((routes.shape[2], count), jnp.float32),
            pltpu.SemaphoreType.DMA((2 + 2 * STREAMS,)),
        ],
        specs=[ANYWHERE] * 3,
    )
    first, second = pieces[::2], pieces[1::2]
    o, i, p = [[None] * 8 for _ in both], [[None] * 8 for _ in both], [None] * 8

    sent = [None, None]

    def swap(k, s, to_outer, to_inner):
        if k == 3:
            o[s][k - 1], to_outer = lax.optimization_barrier((o[s][k - 1], to_outer))
        if k in (5, 6):
            i[s][k - 1], to_inner = lax.optimization_barrier((i[s][k - 1], to_inner))
        if s == 1 and k == 4:
            to_outer, _ = lax.optimization_barrier((to_outer, sent[0]))
        sent[:] = [to_outer, to_inner]
        o[s][k], i[s][k] = outer(to_outer), inner(to_inner)

    for s in both:
        swap(0, s, first[s], first[s])
    weights = run(
        load,
        "load",
        [held(w.shape) for w in weights],
        *weights,
        scratch=[pltpu.SemaphoreType.DMA((3,))],
        specs=[ANYWHERE] * 3,
        work=(0, 6 * weights[0].size),
    )
    i[0][0], *weights = lax.optimization_barrier((i[0][0], *weights))

    def expert(late, given, *own):
        count_all = piece * (STREAMS + len(own))
        return run(
            pass_of(late),
            "expert_pass",
            [held(block)] * STREAMS + ([held((count, width), jnp.float32)] if own else []),
            *(x for s in both for x in given(s)),
            *own,
            *weights,
            work=(6 * count_all * weights[0].size, 6 * weights[0].size),
        )

    def mixed(body, *operands, shape=block):
        return run(body, body.__name__, held(shape), *operands)

    for s in both:
        swap(1, s, mixed(choose, second[s], i[s][0], shape=tagged), o[s][0])
    p[1] = expert(False, lambda s: (o[s][0],) * 4)
    for s in both:
        swap(2, s, mixed(choose, p[1][s], i[s][1], shape=tagged), o[s][1])
    p[2] = expert(False, lambda s: (o[s][1], i[s][0]) * 2)
    for s in both:
        swap(3, s, mixed(choose, p[2][s], i[s][2]), second[s])
    p[3] = expert(False, lambda s: (o[s][2], i[s][1]) * 2)
    for s in both:
        swap(4, s, mixed(choose, p[3][s], i[s][3]), mixed(add, o[s][3], p[2][s]))
    *p[4], total = expert(True, lambda s: (o[s][3], i[s][2], o[s][2], i[s][1]), *pieces)
    for s in both:
        swap(5, s, mixed(choose, p[4][s], second[s]), mixed(add, o[s][4], p[3][s]))
    p[5] = expert(True, lambda s: (o[s][4], i[s][3], o[s][1], i[s][0]))
    for s in both:
        at_outer = mixed(choose_sum, p[5][s], i[s][5], p[1][s])
        swap(6, s, at_outer, mixed(add, o[s][5], p[4][s]))
    firsts = [
        run(finish_first(s), "finish_first", held(block), total, o[s][6], o[s][2], i[s][4])
        for s in both
    ]
    p[6] = expert(True, lambda s: (o[s][5], o[s][1], o[s][0], o[s][0]))
    for s in both:
        at_outer = mixed(choose_sum, p[6][s], i[s][6], p[6][s])
        swap(7, s, at_outer, mixed(add, o[s][6], p[5][s]))
    done = [None] * 4
    for s in both:
        done[2 * s + 1] = run(
            finish_second(s), "finish_second", held(block), total, o[s][7], i[s][7]
        )
        done[2 * s] = firsts[s]

    def joined(body, parts):
        return run(
            body,
            body.__name__,
            jax.ShapeDtypeStruct((count, width), jnp.bfloat16),
            *parts,
            scratch=[pltpu.SemaphoreType.DMA((2 * STREAMS,))],
            out_specs=ANYWHERE,
        )

    count_s = lax.axis_size("section")
    ring = [(s, (s + 1) % count_s) for s in range(count_s)]
    one = run(join_two, "join_two", held((2 * piece, width)), firsts[0], firsts[1])
    back = lax.ppermute(one, "section", ring)
    given = [back, *(lax.ppermute(done[k], "section", ring) for k in (1, 3))]
    handed = joined(join_apart, given)
    return (joined(join, done)[None], handed[None])


def solution(mesh):
    in_specs = (
        P("section", ("expert", "tensor"), None),
        P("section", ("expert", "tensor"), None),
        P("section", ("expert", "tensor"), None),
        P("section", "expert", None, None),
        P("section", "expert", None, None),
        P("section", "expert", None, None),
    )
    out_specs = (P("section", ("expert", "tensor"), None), P("section", ("expert", "tensor"), None))

    def per_device(*args):
        tokens, expert_gate = args[0], args[3]
        line = mesh.shape["expert"] == 4 and mesh.shape["section"] % 2 == 0
        line = line and expert_gate.shape[1] == 1 and tokens.shape[1] == 128
        return (on_line if line else by_slots)(*args)

    return jax.shard_map(
        per_device, mesh=mesh, in_specs=in_specs, out_specs=out_specs, check_vma=False
    )
```

```python
import jax
import jax.numpy as jnp
from jax import lax
from jax.experimental import pallas as pl
from jax.experimental.pallas import tpu as pltpu
from jax.sharding import PartitionSpec as P


def passed_along(value, axis, steps):
    count = lax.axis_size(axis)
    leading, last = (max(0, -steps), min(count, count - steps))
    return lax.ppermute(value, axis, [(source, source + steps) for source in range(leading, last)])


def by_slots(tokens, routes, route_weights, expert_gate, expert_up, expert_down):
    rows_in = tokens[0]
    tok_count, width = rows_in.shape
    top_count = routes.shape[2]
    flat_routes = routes[0].reshape(tok_count * top_count)
    flat_weights = route_weights[0].reshape(tok_count * top_count)
    n_expert = lax.axis_size("expert")
    exp_dev = expert_gate.shape[1]
    expert_count = exp_dev * n_expert
    capacity = max(2, 2 * tok_count * top_count // expert_count)
    onehot = (flat_routes[:, None] == jnp.arange(expert_count, dtype=jnp.int32)[None, :]).astype(
        jnp.int32
    )
    ranked = jnp.sum((jnp.cumsum(onehot, axis=0) - 1) * onehot, axis=1)
    slot_index = flat_routes * capacity + ranked
    token_of = jnp.arange(tok_count * top_count, dtype=jnp.int32) // top_count
    outgoing = (
        jnp.zeros((expert_count * capacity, width), jnp.bfloat16)
        .at[slot_index]
        .set(rows_in[token_of])
    )
    outgoing = outgoing.reshape(n_expert, exp_dev, capacity, width)
    arrived = lax.all_to_all(outgoing, "expert", split_axis=0, concat_axis=2, tiled=True)
    slot_rows = arrived[0]
    gate_val = jnp.einsum(
        "esd,edf->esf", slot_rows, expert_gate[0], preferred_element_type=jnp.float32
    )
    up_val = jnp.einsum("esd,edf->esf", slot_rows, expert_up[0], preferred_element_type=jnp.float32)
    hidden = (jax.nn.silu(gate_val) * up_val).astype(jnp.bfloat16)
    expert_out = jnp.einsum(
        "esf,efd->esd", hidden, expert_down[0], preferred_element_type=jnp.float32
    ).astype(jnp.bfloat16)
    expert_out = expert_out.reshape(exp_dev, n_expert, capacity, width)
    came_back = lax.all_to_all(expert_out, "expert", split_axis=1, concat_axis=0, tiled=True)
    back_rows = came_back.reshape(expert_count * capacity, width)
    picked = back_rows[slot_index].astype(jnp.float32) * flat_weights[:, None]
    routed = jnp.sum(picked.reshape(tok_count, top_count, width), axis=1)
    layer_out = (rows_in.astype(jnp.float32) + routed).astype(jnp.bfloat16)
    handed = passed_along(layer_out, "section", 1)
    return (layer_out[None], handed[None])


TAG = 128
STREAMS = 2
IN_VMEM = pl.BlockSpec(memory_space=pltpu.VMEM)
ANYWHERE = pl.BlockSpec(memory_space=pl.ANY)


def held(shape, dtype=jnp.bfloat16):
    return pltpu.VMEM(shape, dtype)


def wide(ref):
    return ref[...].astype(jnp.float32)


def narrow(value):
    return value.astype(jnp.bfloat16)


def position():
    me = lax.axis_index("expert")
    return me, (me == 0) | (me == 3)


def run(body, name, out_shape, *operands, scratch=(), specs=None, out_specs=None, work=(0, 0)):
    several = isinstance(out_shape, list)
    specs = specs or [IN_VMEM] * len(operands)
    operands = [
        pltpu.with_memory_space_constraint(x, pltpu.VMEM if s is IN_VMEM else pltpu.HBM)
        for x, s in zip(operands, specs)
    ]
    return pl.pallas_call(
        body,
        out_shape=out_shape,
        in_specs=specs,
        out_specs=out_specs or ([IN_VMEM] * len(out_shape) if several else IN_VMEM),
        scratch_shapes=list(scratch),
        compiler_params=pltpu.CompilerParams(vmem_limit_bytes=24 * 2**20),
        cost_estimate=pl.CostEstimate(flops=work[0], bytes_accessed=work[1], transcendentals=0),
        name=name,
    )(*operands)


def prepare(tokens, routes, weights, *refs):
    pieces, (routes_here, weights_here, sems) = refs[: 2 * STREAMS], refs[2 * STREAMS :]
    (count, width), piece = tokens.shape, pieces[0].shape[0]
    moves = [(routes, routes_here), (weights, weights_here)] + [
        (tokens.at[pl.ds(i * piece, piece)], ref if i % 2 else ref.at[:, pl.ds(0, width)])
        for i, ref in enumerate(pieces)
    ]
    copies = [pltpu.make_async_copy(*move, sems.at[i]) for i, move in enumerate(moves)]
    for copy in copies:
        copy.start()
    for copy in copies[:2]:
        copy.wait()
    names = lax.broadcasted_iota(jnp.int32, (8, count), 0)
    rest = jnp.zeros((8, count), jnp.float32)
    for k in range(routes.shape[0]):
        rest += jnp.where(routes_here[k : k + 1, :] == names, weights_here[k : k + 1, :], 0.0)
    parts = []
    for _ in range(3):
        parts.append(narrow(rest).astype(jnp.float32))
        rest = rest - parts[-1]
    parts += [pltpu.roll(part, count - piece, 1) for part in parts]
    parts.append(jnp.zeros((TAG - 48, count), jnp.float32))
    tags = narrow(jnp.concatenate(parts, axis=0).T)
    for copy in copies[2:]:
        copy.wait()
    for s in range(STREAMS):
        pieces[2 * s][:, width:] = tags[2 * s * piece : (2 * s + 1) * piece]


def weight_of(tags, late):
    me, _ = position()
    lane = lax.broadcasted_iota(jnp.int32, tags.shape, 1)
    start = 24 if late else 0
    mine = (lane >= start) & (lane < start + 24) & (lane % 8 == me)
    return jnp.sum(jnp.where(mine, tags.astype(jnp.float32), 0.0), axis=1, keepdims=True)


def expert_of(rows, gate_w, up_w, down_w):
    gate = jnp.dot(rows, gate_w[...], preferred_element_type=jnp.float32)
    up = jnp.dot(rows, up_w[...], preferred_element_type=jnp.float32)
    hidden = narrow(gate / (1.0 + jnp.exp(-gate)) * up)
    out = jnp.dot(hidden, down_w[...], preferred_element_type=jnp.float32)
    return narrow(out).astype(jnp.float32)


def load(*refs):
    sems = refs[6]
    copies = [pltpu.make_async_copy(refs[i], refs[3 + i], sems.at[i]) for i in range(3)]
    for copy in copies:
        copy.start()
    for copy in copies:
        copy.wait()


def pass_of(late):
    def body(*refs):
        _, end = position()
        given, refs = refs[: 4 * STREAMS], refs[4 * STREAMS :]
        pieces = refs[: 2 * STREAMS] if len(refs) > 3 + STREAMS else ()
        refs = refs[len(pieces) :]
        weights, results, totals = refs[:3], refs[3 : 3 + STREAMS], refs[3 + STREAMS :]
        piece, width = results[0].shape
        rows, weight = [], []
        for s in range(STREAMS):
            at_end, at_mid, tag_end, tag_mid = given[4 * s : 4 * s + 4]
            rows.append(jnp.where(end, at_end[:, :width], at_mid[:, :width]))
            weight.append(weight_of(jnp.where(end, tag_end[:, width:], tag_mid[:, width:]), late))
        for i, ref in enumerate(pieces):
            rows.append(ref[:, :width])
            weight.append(weight_of(pieces[i // 2 * 2][:, width:], i % 2))
        rows, weight = jnp.concatenate(rows, axis=0), jnp.concatenate(weight, axis=0)
        out = expert_of(rows, *weights) * weight
        for s in range(STREAMS):
            results[s][...] = narrow(out[s * piece : (s + 1) * piece])
        for total in totals:
            start = STREAMS * piece
            total[...] = rows[start:].astype(jnp.float32) + out[start:]

    return body


def choose(at_end, at_mid, result):
    _, end = position()
    width = min(at_end.shape[1], at_mid.shape[1], result.shape[1])
    result[:, :width] = jnp.where(end, at_end[:, :width], at_mid[:, :width])
    if result.shape[1] > width:
        wider, here = (at_mid, ~end) if at_mid.shape[1] > width else (at_end, end)
        rest = wider[:, width:]
        result[:, width:] = jnp.where(here, rest, jnp.zeros_like(rest))


def choose_sum(at_end, mid_a, mid_b, result):
    _, end = position()
    result[...] = jnp.where(end, at_end[...], narrow(wide(mid_a) + wide(mid_b)))


def add(a, b, result):
    result[...] = narrow(wide(a) + wide(b))


def finish_first(stream):
    def body(total, far, near, inner, result):
        _, end = position()
        piece, width = result.shape
        own = total[2 * stream * piece : (2 * stream + 1) * piece]
        at_mid = near[:, :width].astype(jnp.float32) + wide(inner)
        result[...] = narrow(own + jnp.where(end, wide(far), at_mid))

    return body


def finish_second(stream):
    def body(total, outer, inner, result):
        _, end = position()
        piece = result.shape[0]
        own = total[(2 * stream + 1) * piece : (2 * stream + 2) * piece]
        result[...] = narrow(own + wide(outer) + jnp.where(end, 0.0, wide(inner)))

    return body


def join(*refs):
    parts, whole, sems = refs[:-2], refs[-2], refs[-1]
    copies, row = [], 0
    for i, part in enumerate(parts):
        there = whole.at[pl.ds(row, part.shape[0])]
        copies.append(pltpu.make_async_copy(part, there, sems.at[i]))
        row += part.shape[0]
    for copy in copies:
        copy.start()
    for copy in copies:
        copy.wait()


def join_two(a, b, result):
    half = a.shape[0]
    result[:half] = a[...]
    result[half:] = b[...]


def join_handed(firsts, *refs):
    seconds, (whole, zeros, sems) = refs[:STREAMS], refs[STREAMS:]
    piece = seconds[0].shape[0]
    nothing = lax.axis_index("section") == 0

    @pl.when(nothing)
    def _():
        zeros[...] = jnp.zeros_like(zeros)
        join(*[zeros] * (2 * STREAMS), whole, sems)

    @pl.when(~nothing)
    def _():
        parts = []
        for s in range(STREAMS):
            parts += [firsts.at[pl.ds(s * piece, piece)], seconds[s]]
        join(*parts, whole, sems)


def on_line(tokens, routes, route_weights, expert_gate, expert_up, expert_down):
    rows = tokens[0]
    count, width = rows.shape
    piece = count // (2 * STREAMS)
    block = (piece, width)
    both = range(STREAMS)
    weights = (expert_gate[0, 0], expert_up[0, 0], expert_down[0, 0])
    axes = ("section", "expert")
    sections = range(lax.axis_size("section"))
    outer_pairs = [(s * 4 + e, s * 4 + (e ^ 1)) for s in sections for e in range(4)]
    inner_pairs = [
        (s * 4 + e, s * 4 + 3 - e if e in (1, 2) else (s ^ 1) * 4 + e)
        for s in sections
        for e in range(4)
    ]

    def outer(value):
        return lax.ppermute(value, axes, outer_pairs)

    def inner(value):
        return lax.ppermute(value, axes, inner_pairs)

    tagged = (piece, width + TAG)
    pieces = run(
        prepare,
        "prepare",
        [held(tagged), held(block)] * STREAMS,
        rows,
        routes[0].T,
        route_weights[0].T,
        scratch=[
            held((routes.shape[2], count), jnp.int32),
            held((routes.shape[2], count), jnp.float32),
            pltpu.SemaphoreType.DMA((2 + 2 * STREAMS,)),
        ],
        specs=[ANYWHERE] * 3,
    )
    first, second = pieces[::2], pieces[1::2]
    o, i, p = [[None] * 8 for _ in both], [[None] * 8 for _ in both], [None] * 8

    sent = [None, None]

    def swap(k, s, to_outer, to_inner):
        if k == 3:
            o[s][k - 1], to_outer = lax.optimization_barrier((o[s][k - 1], to_outer))
        if k in (5, 6, 7):
            i[s][k - 1], to_inner = lax.optimization_barrier((i[s][k - 1], to_inner))
        if k == 7:
            to_outer, to_inner = lax.optimization_barrier((to_outer, to_inner))
        sent[:] = [to_outer, to_inner]
        o[s][k], i[s][k] = outer(to_outer), inner(to_inner)

    for s in both:
        swap(0, s, first[s], first[s])
    weights = run(
        load,
        "load",
        [held(w.shape) for w in weights],
        *weights,
        scratch=[pltpu.SemaphoreType.DMA((3,))],
        specs=[ANYWHERE] * 3,
        work=(0, 6 * weights[0].size),
    )
    i[0][0], *weights = lax.optimization_barrier((i[0][0], *weights))

    def expert(late, given, *own):
        count_all = piece * (STREAMS + len(own))
        return run(
            pass_of(late),
            "expert_pass",
            [held(block)] * STREAMS + ([held((count, width), jnp.float32)] if own else []),
            *(x for s in both for x in given(s)),
            *own,
            *weights,
            work=(6 * count_all * weights[0].size, 6 * weights[0].size),
        )

    def mixed(body, *operands, shape=block):
        return run(body, body.__name__, held(shape), *operands)

    for s in both:
        swap(1, s, mixed(choose, second[s], i[s][0], shape=tagged), o[s][0])
    p[1] = expert(False, lambda s: (o[s][0],) * 4)
    for s in both:
        swap(2, s, mixed(choose, p[1][s], i[s][1], shape=tagged), o[s][1])
    *p[2], total = expert(False, lambda s: (o[s][1], i[s][0]) * 2, *pieces)
    for s in both:
        swap(3, s, mixed(choose, p[2][s], i[s][2]), second[s])
    p[3] = expert(False, lambda s: (o[s][2], i[s][1]) * 2)
    for s in both:
        swap(4, s, mixed(choose, p[3][s], i[s][3]), mixed(add, o[s][3], p[2][s]))
    o[1][3], _ = lax.optimization_barrier((o[1][3], sent[1]))
    p[4] = expert(True, lambda s: (o[s][3], i[s][2], o[s][2], i[s][1]))
    for s in both:
        swap(5, s, mixed(choose, p[4][s], second[s]), mixed(add, o[s][4], p[3][s]))
    p[5] = expert(True, lambda s: (o[s][4], i[s][3], o[s][1], i[s][0]))
    for s in both:
        at_outer = mixed(choose_sum, p[5][s], i[s][5], p[1][s])
        swap(6, s, at_outer, mixed(add, o[s][5], p[4][s]))
    firsts = [
        run(finish_first(s), "finish_first", held(block), total, o[s][6], o[s][2], i[s][4])
        for s in both
    ]
    p[6] = expert(True, lambda s: (o[s][5], o[s][1], o[s][0], o[s][0]))
    for s in both:
        at_outer = mixed(choose_sum, p[6][s], i[s][6], p[6][s])
        swap(7, s, at_outer, mixed(add, o[s][6], p[5][s]))
    done = [None] * 4
    for s in both:
        done[2 * s + 1] = run(
            finish_second(s), "finish_second", held(block), total, o[s][7], i[s][7]
        )
        done[2 * s] = firsts[s]

    def joined(body, parts, *scratch):
        return run(
            body,
            body.__name__,
            jax.ShapeDtypeStruct((count, width), jnp.bfloat16),
            *parts,
            scratch=[*scratch, pltpu.SemaphoreType.DMA((2 * STREAMS,))],
            out_specs=ANYWHERE,
        )

    count_s = lax.axis_size("section")
    ring = [(s, (s + 1) % count_s) for s in range(count_s)]
    one = run(join_two, "join_two", held((2 * piece, width)), firsts[0], firsts[1])
    back = lax.ppermute(one, "section", ring)
    given = [back, *(lax.ppermute(done[k], "section", ring) for k in (1, 3))]
    handed = joined(join_handed, given, held(block))
    return (joined(join, done)[None], handed[None])


def solution(mesh):
    in_specs = (
        P("section", ("expert", "tensor"), None),
        P("section", ("expert", "tensor"), None),
        P("section", ("expert", "tensor"), None),
        P("section", "expert", None, None),
        P("section", "expert", None, None),
        P("section", "expert", None, None),
    )
    out_specs = (P("section", ("expert", "tensor"), None), P("section", ("expert", "tensor"), None))

    def per_device(*args):
        tokens, expert_gate = args[0], args[3]
        line = mesh.shape["expert"] == 4 and mesh.shape["section"] % 2 == 0
        line = line and expert_gate.shape[1] == 1 and tokens.shape[1] == 128
        return (on_line if line else by_slots)(*args)

    return jax.shard_map(
        per_device, mesh=mesh, in_specs=in_specs, out_specs=out_specs, check_vma=False
    )
```

```python
import jax
import jax.numpy as jnp
from jax import lax
from jax.experimental import pallas as pl
from jax.experimental.pallas import tpu as pltpu
from jax.sharding import PartitionSpec as P


def passed_along(value, axis, steps):
    count = lax.axis_size(axis)
    leading, last = (max(0, -steps), min(count, count - steps))
    return lax.ppermute(value, axis, [(source, source + steps) for source in range(leading, last)])


def by_slots(tokens, routes, route_weights, expert_gate, expert_up, expert_down):
    rows_in = tokens[0]
    tok_count, width = rows_in.shape
    top_count = routes.shape[2]
    flat_routes = routes[0].reshape(tok_count * top_count)
    flat_weights = route_weights[0].reshape(tok_count * top_count)
    n_expert = lax.axis_size("expert")
    exp_dev = expert_gate.shape[1]
    expert_count = exp_dev * n_expert
    capacity = max(2, 2 * tok_count * top_count // expert_count)
    onehot = (flat_routes[:, None] == jnp.arange(expert_count, dtype=jnp.int32)[None, :]).astype(
        jnp.int32
    )
    ranked = jnp.sum((jnp.cumsum(onehot, axis=0) - 1) * onehot, axis=1)
    slot_index = flat_routes * capacity + ranked
    token_of = jnp.arange(tok_count * top_count, dtype=jnp.int32) // top_count
    outgoing = (
        jnp.zeros((expert_count * capacity, width), jnp.bfloat16)
        .at[slot_index]
        .set(rows_in[token_of])
    )
    outgoing = outgoing.reshape(n_expert, exp_dev, capacity, width)
    arrived = lax.all_to_all(outgoing, "expert", split_axis=0, concat_axis=2, tiled=True)
    slot_rows = arrived[0]
    gate_val = jnp.einsum(
        "esd,edf->esf", slot_rows, expert_gate[0], preferred_element_type=jnp.float32
    )
    up_val = jnp.einsum("esd,edf->esf", slot_rows, expert_up[0], preferred_element_type=jnp.float32)
    hidden = (jax.nn.silu(gate_val) * up_val).astype(jnp.bfloat16)
    expert_out = jnp.einsum(
        "esf,efd->esd", hidden, expert_down[0], preferred_element_type=jnp.float32
    ).astype(jnp.bfloat16)
    expert_out = expert_out.reshape(exp_dev, n_expert, capacity, width)
    came_back = lax.all_to_all(expert_out, "expert", split_axis=1, concat_axis=0, tiled=True)
    back_rows = came_back.reshape(expert_count * capacity, width)
    picked = back_rows[slot_index].astype(jnp.float32) * flat_weights[:, None]
    routed = jnp.sum(picked.reshape(tok_count, top_count, width), axis=1)
    layer_out = (rows_in.astype(jnp.float32) + routed).astype(jnp.bfloat16)
    handed = passed_along(layer_out, "section", 1)
    return (layer_out[None], handed[None])


TAG = 128
STREAMS = 2
IN_VMEM = pl.BlockSpec(memory_space=pltpu.VMEM)
ANYWHERE = pl.BlockSpec(memory_space=pl.ANY)


def held(shape, dtype=jnp.bfloat16):
    return pltpu.VMEM(shape, dtype)


def wide(ref):
    return ref[...].astype(jnp.float32)


def narrow(value):
    return value.astype(jnp.bfloat16)


def position():
    me = lax.axis_index("expert")
    return me, (me == 0) | (me == 3)


def run(body, name, out_shape, *operands, scratch=(), specs=None, out_specs=None, work=(0, 0), alias=()):
    several = isinstance(out_shape, list)
    specs = specs or [IN_VMEM] * len(operands)
    operands = [
        pltpu.with_memory_space_constraint(x, pltpu.VMEM if s is IN_VMEM else pltpu.HBM)
        for x, s in zip(operands, specs)
    ]
    return pl.pallas_call(
        body,
        out_shape=out_shape,
        in_specs=specs,
        out_specs=out_specs or ([IN_VMEM] * len(out_shape) if several else IN_VMEM),
        scratch_shapes=list(scratch),
        compiler_params=pltpu.CompilerParams(vmem_limit_bytes=24 * 2**20),
        cost_estimate=pl.CostEstimate(flops=work[0], bytes_accessed=work[1], transcendentals=0),
        input_output_aliases=dict(alias),
        name=name,
    )(*operands)


def prepare(tokens, routes, weights, *refs):
    pieces, (routes_here, weights_here, sems) = refs[: 2 * STREAMS], refs[2 * STREAMS :]
    (count, width), piece = tokens.shape, pieces[0].shape[0]
    moves = [(routes, routes_here), (weights, weights_here)] + [
        (tokens.at[pl.ds(i * piece, piece)], ref if i % 2 else ref.at[:, pl.ds(0, width)])
        for i, ref in enumerate(pieces)
    ]
    copies = [pltpu.make_async_copy(*move, sems.at[i]) for i, move in enumerate(moves)]
    for copy in copies:
        copy.start()
    for copy in copies[:2]:
        copy.wait()
    names = lax.broadcasted_iota(jnp.int32, (8, count), 0)
    rest = jnp.zeros((8, count), jnp.float32)
    for k in range(routes.shape[0]):
        rest += jnp.where(routes_here[k : k + 1, :] == names, weights_here[k : k + 1, :], 0.0)
    parts = []
    for _ in range(3):
        parts.append(narrow(rest).astype(jnp.float32))
        rest = rest - parts[-1]
    parts += [pltpu.roll(part, count - piece, 1) for part in parts]
    parts.append(jnp.zeros((TAG - 48, count), jnp.float32))
    tags = narrow(jnp.concatenate(parts, axis=0).T)
    for copy in copies[2:]:
        copy.wait()
    for s in range(STREAMS):
        pieces[2 * s][:, width:] = tags[2 * s * piece : (2 * s + 1) * piece]


def weight_of(tags, late):
    me, _ = position()
    lane = lax.broadcasted_iota(jnp.int32, tags.shape, 1)
    start = 24 if late else 0
    mine = (lane >= start) & (lane < start + 24) & (lane % 8 == me)
    return jnp.sum(jnp.where(mine, tags.astype(jnp.float32), 0.0), axis=1, keepdims=True)


def expert_of(rows, gate_w, up_w, down_w):
    gate = jnp.dot(rows, gate_w[...], preferred_element_type=jnp.float32)
    up = jnp.dot(rows, up_w[...], preferred_element_type=jnp.float32)
    hidden = narrow(gate / (1.0 + jnp.exp(-gate)) * up)
    out = jnp.dot(hidden, down_w[...], preferred_element_type=jnp.float32)
    return narrow(out).astype(jnp.float32)


def load(*refs):
    sems = refs[6]
    copies = [pltpu.make_async_copy(refs[i], refs[3 + i], sems.at[i]) for i in range(3)]
    for copy in copies:
        copy.start()
    for copy in copies:
        copy.wait()


def pass_of(late):
    def body(*refs):
        _, end = position()
        given, refs = refs[: 4 * STREAMS], refs[4 * STREAMS :]
        pieces = refs[: 2 * STREAMS] if len(refs) > 3 + STREAMS else ()
        refs = refs[len(pieces) :]
        weights, results, totals = refs[:3], refs[3 : 3 + STREAMS], refs[3 + STREAMS :]
        piece, width = results[0].shape
        rows, weight = [], []
        for s in range(STREAMS):
            at_end, at_mid, tag_end, tag_mid = given[4 * s : 4 * s + 4]
            rows.append(jnp.where(end, at_end[:, :width], at_mid[:, :width]))
            weight.append(weight_of(jnp.where(end, tag_end[:, width:], tag_mid[:, width:]), late))
        for i, ref in enumerate(pieces):
            rows.append(ref[:, :width])
            weight.append(weight_of(pieces[i // 2 * 2][:, width:], i % 2))
        rows, weight = jnp.concatenate(rows, axis=0), jnp.concatenate(weight, axis=0)
        out = expert_of(rows, *weights) * weight
        for s in range(STREAMS):
            results[s][...] = narrow(out[s * piece : (s + 1) * piece])
        for total in totals:
            start = STREAMS * piece
            total[...] = rows[start:].astype(jnp.float32) + out[start:]

    return body


def choose(at_end, at_mid, result):
    _, end = position()
    width = min(at_end.shape[1], at_mid.shape[1], result.shape[1])
    result[:, :width] = jnp.where(end, at_end[:, :width], at_mid[:, :width])
    if result.shape[1] > width:
        wider, here = (at_mid, ~end) if at_mid.shape[1] > width else (at_end, end)
        rest = wider[:, width:]
        result[:, width:] = jnp.where(here, rest, jnp.zeros_like(rest))


def choose_sum(at_end, mid_a, mid_b, result):
    _, end = position()
    result[...] = jnp.where(end, at_end[...], narrow(wide(mid_a) + wide(mid_b)))


def add(a, b, result):
    result[...] = narrow(wide(a) + wide(b))


def finish_first(stream):
    def body(total, far, near, inner, result):
        _, end = position()
        piece, width = result.shape
        own = total[2 * stream * piece : (2 * stream + 1) * piece]
        at_mid = near[:, :width].astype(jnp.float32) + wide(inner)
        result[...] = narrow(own + jnp.where(end, wide(far), at_mid))

    return body


def finish_second(stream):
    def body(total, outer, inner, result):
        _, end = position()
        piece = result.shape[0]
        own = total[(2 * stream + 1) * piece : (2 * stream + 2) * piece]
        result[...] = narrow(own + wide(outer) + jnp.where(end, 0.0, wide(inner)))

    return body


def join(*refs):
    parts, whole, sems = refs[:-2], refs[-2], refs[-1]
    copies, row = [], 0
    for i, part in enumerate(parts):
        there = whole.at[pl.ds(row, part.shape[0])]
        copies.append(pltpu.make_async_copy(part, there, sems.at[i]))
        row += part.shape[0]
    for copy in copies:
        copy.start()
    for copy in copies:
        copy.wait()


def join_two(a, b, result):
    half = a.shape[0]
    result[:half] = a[...]
    result[half:] = b[...]


def join_handed(firsts, early, whole, zeros, sems):
    piece = early.shape[0]
    nothing = lax.axis_index("section") == 0
    places = [(firsts.at[pl.ds(s * piece, piece)], 2 * s) for s in range(STREAMS)] + [(early, 1)]

    def put(parts):
        copies = [
            pltpu.make_async_copy(part, whole.at[pl.ds(place * piece, piece)], sems.at[place])
            for part, place in parts
        ]
        for copy in copies:
            copy.start()
        for copy in copies:
            copy.wait()

    @pl.when(nothing)
    def _():
        zeros[...] = jnp.zeros_like(zeros)
        put([(zeros, place) for _, place in places])

    @pl.when(~nothing)
    def _():
        put(places)


def join_last(begun, last, whole, zeros, sems):
    piece = last.shape[0]
    there = whole.at[pl.ds(whole.shape[0] - piece, piece)]
    nothing = lax.axis_index("section") == 0

    @pl.when(nothing)
    def _():
        zeros[...] = jnp.zeros_like(zeros)

    @pl.when(~nothing)
    def _():
        zeros[...] = last[...]

    copy = pltpu.make_async_copy(zeros, there, sems.at[0])
    copy.start()
    copy.wait()


def on_line(tokens, routes, route_weights, expert_gate, expert_up, expert_down):
    rows = tokens[0]
    count, width = rows.shape
    piece = count // (2 * STREAMS)
    block = (piece, width)
    both = range(STREAMS)
    weights = (expert_gate[0, 0], expert_up[0, 0], expert_down[0, 0])
    axes = ("section", "expert")
    sections = range(lax.axis_size("section"))
    outer_pairs = [(s * 4 + e, s * 4 + (e ^ 1)) for s in sections for e in range(4)]
    inner_pairs = [
        (s * 4 + e, s * 4 + 3 - e if e in (1, 2) else (s ^ 1) * 4 + e)
        for s in sections
        for e in range(4)
    ]

    def outer(value):
        return lax.ppermute(value, axes, outer_pairs)

    def inner(value):
        return lax.ppermute(value, axes, inner_pairs)

    tagged = (piece, width + TAG)
    pieces = run(
        prepare,
        "prepare",
        [held(tagged), held(block)] * STREAMS,
        rows,
        routes[0].T,
        route_weights[0].T,
        scratch=[
            held((routes.shape[2], count), jnp.int32),
            held((routes.shape[2], count), jnp.float32),
            pltpu.SemaphoreType.DMA((2 + 2 * STREAMS,)),
        ],
        specs=[ANYWHERE] * 3,
    )
    first, second = pieces[::2], pieces[1::2]
    o, i, p = [[None] * 8 for _ in both], [[None] * 8 for _ in both], [None] * 8

    sent = [None, None]

    def swap(k, s, to_outer, to_inner):
        if k == 3:
            o[s][k - 1], to_outer = lax.optimization_barrier((o[s][k - 1], to_outer))
        if k in (5, 6, 7):
            i[s][k - 1], to_inner = lax.optimization_barrier((i[s][k - 1], to_inner))
        if k == 7:
            to_outer, to_inner = lax.optimization_barrier((to_outer, to_inner))
        sent[:] = [to_outer, to_inner]
        o[s][k], i[s][k] = outer(to_outer), inner(to_inner)

    for s in both:
        swap(0, s, first[s], first[s])
    weights = run(
        load,
        "load",
        [held(w.shape) for w in weights],
        *weights,
        scratch=[pltpu.SemaphoreType.DMA((3,))],
        specs=[ANYWHERE] * 3,
        work=(0, 6 * weights[0].size),
    )
    i[0][0], *weights = lax.optimization_barrier((i[0][0], *weights))

    def expert(late, given, *own):
        count_all = piece * (STREAMS + len(own))
        return run(
            pass_of(late),
            "expert_pass",
            [held(block)] * STREAMS + ([held((count, width), jnp.float32)] if own else []),
            *(x for s in both for x in given(s)),
            *own,
            *weights,
            work=(6 * count_all * weights[0].size, 6 * weights[0].size),
        )

    def mixed(body, *operands, shape=block):
        return run(body, body.__name__, held(shape), *operands)

    for s in both:
        swap(1, s, mixed(choose, second[s], i[s][0], shape=tagged), o[s][0])
    p[1] = expert(False, lambda s: (o[s][0],) * 4)
    for s in both:
        swap(2, s, mixed(choose, p[1][s], i[s][1], shape=tagged), o[s][1])
    *p[2], total = expert(False, lambda s: (o[s][1], i[s][0]) * 2, *pieces)
    for s in both:
        swap(3, s, mixed(choose, p[2][s], i[s][2]), second[s])
    p[3] = expert(False, lambda s: (o[s][2], i[s][1]) * 2)
    for s in both:
        swap(4, s, mixed(choose, p[3][s], i[s][3]), mixed(add, o[s][3], p[2][s]))
    o[1][3], _ = lax.optimization_barrier((o[1][3], sent[1]))
    p[4] = expert(True, lambda s: (o[s][3], i[s][2], o[s][2], i[s][1]))
    for s in both:
        swap(5, s, mixed(choose, p[4][s], second[s]), mixed(add, o[s][4], p[3][s]))
    p[5] = expert(True, lambda s: (o[s][4], i[s][3], o[s][1], i[s][0]))
    for s in both:
        at_outer = mixed(choose_sum, p[5][s], i[s][5], p[1][s])
        swap(6, s, at_outer, mixed(add, o[s][5], p[4][s]))
    firsts = [
        run(finish_first(s), "finish_first", held(block), total, o[s][6], o[s][2], i[s][4])
        for s in both
    ]
    p[6] = expert(True, lambda s: (o[s][5], o[s][1], o[s][0], o[s][0]))
    for s in both:
        at_outer = mixed(choose_sum, p[6][s], i[s][6], p[6][s])
        swap(7, s, at_outer, mixed(add, o[s][6], p[5][s]))
    done = [None] * 4
    for s in both:
        done[2 * s + 1] = run(
            finish_second(s), "finish_second", held(block), total, o[s][7], i[s][7]
        )
        done[2 * s] = firsts[s]

    def joined(body, parts, *scratch):
        return run(
            body,
            body.__name__,
            jax.ShapeDtypeStruct((count, width), jnp.bfloat16),
            *parts,
            scratch=[*scratch, pltpu.SemaphoreType.DMA((2 * STREAMS,))],
            out_specs=ANYWHERE,
        )

    count_s = lax.axis_size("section")
    ring = [(s, (s + 1) % count_s) for s in range(count_s)]
    one = run(join_two, "join_two", held((2 * piece, width)), firsts[0], firsts[1])
    back = lax.ppermute(one, "section", ring)
    given = [back, *(lax.ppermute(done[k], "section", ring) for k in (1, 3))]
    begun = joined(join_handed, given[:2], held(block))
    handed = run(
        join_last,
        "join_last",
        jax.ShapeDtypeStruct((count, width), jnp.bfloat16),
        begun,
        given[2],
        scratch=[held(block), pltpu.SemaphoreType.DMA((1,))],
        specs=[ANYWHERE, IN_VMEM],
        out_specs=ANYWHERE,
        alias=[(0, 0)],
    )
    return (joined(join, done)[None], handed[None])


def solution(mesh):
    in_specs = (
        P("section", ("expert", "tensor"), None),
        P("section", ("expert", "tensor"), None),
        P("section", ("expert", "tensor"), None),
        P("section", "expert", None, None),
        P("section", "expert", None, None),
        P("section", "expert", None, None),
    )
    out_specs = (P("section", ("expert", "tensor"), None), P("section", ("expert", "tensor"), None))

    def per_device(*args):
        tokens, expert_gate = args[0], args[3]
        line = mesh.shape["expert"] == 4 and mesh.shape["section"] % 2 == 0
        line = line and expert_gate.shape[1] == 1 and tokens.shape[1] == 128
        return (on_line if line else by_slots)(*args)

    return jax.shard_map(
        per_device, mesh=mesh, in_specs=in_specs, out_specs=out_specs, check_vma=False
    )
```
